512 devices in a mesh: dp: 64 (over z, y_lo, core), mp: 8 (over y_hi, x).
Axes of the slice: x: 4, y: 8 (y_hi: 2, y_lo: 4; y = y_hi * 4 + y_lo), z: 8, core: 2. Of those that a mesh axis runs over, the one named last changes fastest.
Arguments:
- acts: bfloat16 [32768, 12288], P('dp', 'mp'), may hold values from -8 to 8
- lengths: int32 [128], P('dp'), may hold values from 1 to 256, as said below
- ln_gain: float32 [12288], P('mp'), may hold values from 0.1 to 1.9
- ln_bias: float32 [12288], P('mp'), may hold values from -3 to 3
- w_fc1: bfloat16 [12288, 24576], P('dp', 'mp'), may hold values from -0.0546875 to 0.0546875
Outputs:
- w_served: bfloat16 [24576, 12288], P(('mp', 'dp'))
- scales: float32 [12288], P('mp')
- tok_scale: float32 [32768], P('dp')
The draws below stay inside these ranges and needn't reach their ends.
Inputs may be any that keep to these rules, and one draw needn't show every extreme that they name: `lengths`: in every draw some sequence has all 256 positions valid and some has one.
All inputs are finite; a program needn't handle non-finite values. Where the reference program divides by a largest or mean magnitude, that divisor is 1e-20 or more.
Results may differ from the reference program's by a relative error of at most 0.0004.
Values may be sent and summed in bfloat16 or wider, within the bound.
No kernel may reach another device: no remote copies, remote signals or barrier semaphores. Data moves between devices by JAX's collectives and lax.ppermute only.
A program may use at most 64 MiB of HBM per device.

```python
import jax
import jax.numpy as jnp
from jax import lax

D = 12288
FFW = 24576
SLOT = 256
SEQS = 128
TOKENS = 32768


def draw_lengths(key, part):
    key = jax.random.fold_in(key, 7)
    first, second, third = jax.random.split(key, 3)
    drawn = jax.random.randint(first, (SEQS,), 1, SLOT + 1)
    top_slot = jax.random.randint(second, (), 0, SEQS)
    low_slot = (top_slot + 1 + jax.random.randint(third, (), 0, SEQS - 1)) % SEQS
    places = jnp.arange(SEQS)
    drawn = jnp.where(places == top_slot, SLOT, drawn)
    drawn = jnp.where(places == low_slot, 1, drawn)
    return drawn.astype(jnp.int32)


def raised(values, key, source, target, shards_of, factor):
    owner, partner = [(jnp.arange(values.shape[dim]) // (values.shape[dim] // shards_of)).reshape([-1 if axis == dim else 1 for axis in range(values.ndim)]) for dim in (source, target)]
    chosen = jax.random.permutation(key, shards_of)[partner]
    strong = (owner == chosen) | (owner == (partner + shards_of // 2) % shards_of)
    return jnp.where(strong, factor * values, values)


def block_levels(own_key, shape, pieces, smallest, largest):
    def one(position, shards_of):
        draws = jax.random.uniform(jax.random.fold_in(jax.random.fold_in(own_key, 6), position), (shards_of,), jnp.float32, smallest / len(pieces), largest / len(pieces))
        return jnp.repeat(jnp.exp(draws), shape[position] // shards_of).reshape((-1,) + (1,) * (len(shape) - position - 1))

    factor_of = one(*pieces[0])
    for cut in pieces[1:]:
        factor_of = factor_of * one(*cut)
    return factor_of


def normal_values(rng, extent, spread, reach, cuts=(), held_as=jnp.bfloat16):
    array = jax.random.normal(rng, extent, jnp.float32) * spread
    if len(cuts) > 0:
        array = block_levels(rng, extent, cuts, -0.22, 0.18) * array
    return jnp.clip(array, min=-reach, max=reach).astype(held_as)


def noise_with(stream_key, dims, width, bound, shards, heavy, kind=jnp.bfloat16):
    values = width * jax.random.normal(stream_key, dims, jnp.float32)
    if shards:
        values = values * block_levels(stream_key, dims, shards, -0.22, 0.18)
    return jnp.clip(raised(values, jax.random.fold_in(stream_key, 3), *heavy), -bound, bound).astype(kind)


def setup_inputs(seed: int = 0) -> dict:
    keys = jax.random.split(jax.random.key(seed), 6)
    acts = noise_with(keys[0], (TOKENS, D), 1.0, 8.0, ((0, 64), (1, 8)), (0, 1, 64, 4.0))
    lengths = draw_lengths(jax.random.fold_in(keys[5], 71), 0)
    ln_gain = jnp.clip(1.0 + 0.18 * jax.random.normal(keys[2], (D,), jnp.float32), 0.1, 1.9)
    ln_bias = normal_values(keys[3], (D,), 0.5, 3.0, ((0, 8),), jnp.float32)
    w_fc1 = normal_values(keys[4], (D, FFW), D ** -0.5, 0.0546875, ((0, 64), (1, 8)))
    return dict(acts=acts, lengths=lengths, ln_gain=ln_gain, ln_bias=ln_bias, w_fc1=w_fc1)


def reference(acts, lengths, ln_gain, ln_bias, w_fc1):
    x = acts.astype(jnp.float32)
    mean = lax.optimization_barrier(jnp.sum(x, axis=1)) / D
    var = lax.optimization_barrier(jnp.sum(x * x, axis=1)) / D - mean * mean
    normed = (x - mean[:, None]) * lax.rsqrt(var + 1e-05)[:, None] * ln_gain + ln_bias
    positions = lax.broadcasted_iota(jnp.int32, (SEQS, SLOT), 1)
    valid = (positions < lengths[:, None]).reshape(TOKENS)
    act_max = lax.optimization_barrier(jnp.max(jnp.where(valid[:, None], jnp.abs(normed), 0.0), axis=0))
    w_max = lax.optimization_barrier(jnp.max(jnp.abs(w_fc1.astype(jnp.float32)), axis=1))
    scales = jnp.sqrt(act_max + 1e-05) / jnp.sqrt(w_max + 1e-05)
    w_served = (w_fc1.astype(jnp.float32) * scales[:, None]).astype(jnp.bfloat16).T
    peaks = lax.optimization_barrier(jnp.max(jnp.abs(normed / scales), axis=1))
    tok_scale = jnp.where(valid, peaks, 0.0)
    return (w_served, scales, tok_scale)
```

```python
import jax
import jax.numpy as jnp
from jax import lax
from jax.experimental import pallas as pl
from jax.experimental.pallas import tpu as pltpu
from jax.sharding import PartitionSpec as P

D = 12288
SLOT = 256
EPS = 1e-05
VMEM_SPEC = pl.BlockSpec(memory_space=pltpu.VMEM)
SMEM_SPEC = pl.BlockSpec(memory_space=pltpu.SMEM)


def params():
    return pltpu.CompilerParams(vmem_limit_bytes=40 * 1024 * 1024)


def stats_kernel(place_ref, acts_ref, w_ref, page_ref, rows_ref):
    parity = place_ref[0] % 2
    for block in range(4):
        total = jnp.zeros((128, 128), jnp.float32)
        square = jnp.zeros((128, 128), jnp.float32)
        for tile in range(12):
            x = acts_ref[pl.ds(128 * block, 128), pl.ds(128 * tile, 128)].astype(jnp.float32)
            total = total + x
            square = square + x * x
        page_ref[0, block : block + 1, :] = jnp.sum(total.T, axis=0, keepdims=True)
        page_ref[0, 4 + block : 5 + block, :] = jnp.sum(square.T, axis=0, keepdims=True)
    rows_ref[...] = jnp.zeros_like(rows_ref)
    for part in range(2):
        peak = jnp.zeros((96, 128), jnp.float32)
        for tile in range(24):
            peak = jnp.maximum(peak, jnp.abs(w_ref[pl.ds(96 * part, 96), pl.ds(128 * tile, 128)].astype(jnp.float32)))
        rows_ref[pl.ds(pl.multiple_of(192 * parity + 96 * part, 32), 96), :] = peak
    for block in range(3):
        page_ref[0, 8 + block : 9 + block, :] = jnp.max(rows_ref[pl.ds(128 * block, 128), :].T, axis=0, keepdims=True)
    page_ref[0, 11:16, :] = jnp.zeros((5, 128), jnp.float32)
    page = page_ref[0]
    for peer in range(1, page_ref.shape[0]):
        page_ref[peer] = page


def pack_kernel(place_ref, w_ref, page_ref):
    parity = place_ref[0] % 2
    low = lax.broadcasted_iota(jnp.int32, (24, 128), 1) < 64
    first = low == (parity == 0)

    def step(index, carry):
        columns = pl.ds(pl.multiple_of(384 * index, 128), 384)
        full = w_ref[pl.ds(pl.multiple_of(64 * parity, 64), 128), columns].astype(jnp.float32).T
        half = w_ref[pl.ds(pl.multiple_of(128 * (1 - parity), 64), 64), columns].astype(jnp.float32)
        twice = jnp.concatenate([half, half], axis=0).T
        for peer in range(8):
            upper = twice[48 * peer : 48 * peer + 24]
            lower = twice[48 * peer + 24 : 48 * peer + 48]
            page = jnp.concatenate([full[48 * peer : 48 * peer + 48], jnp.where(first, upper, lower)], axis=0)
            page_ref[8 * index + peer] = page.astype(jnp.bfloat16)
        return carry

    lax.fori_loop(0, 8, step, 0)


def moments(sums):
    total = jnp.sum(sums[:, 0:8], axis=0)
    mean = total[0:4] / D
    var = total[4:8] / D - mean * mean
    rstd = lax.rsqrt(var + EPS)
    return jnp.concatenate([mean, rstd], axis=0).T


def act_kernel(lengths_ref, sums_ref, acts_ref, gain_ref, bias_ref, page_ref):
    columns = moments(sums_ref[...])
    place = lax.broadcasted_iota(jnp.int32, (128, 1), 0)
    for tile in range(12):
        gain = gain_ref[tile : tile + 1, :]
        bias = bias_ref[tile : tile + 1, :]
        peak = jnp.zeros((128, 128), jnp.float32)
        for block in range(4):
            x = acts_ref[pl.ds(128 * block, 128), pl.ds(128 * tile, 128)].astype(jnp.float32)
            normed = (x - columns[:, block : block + 1]) * columns[:, 4 + block : 5 + block] * gain + bias
            valid = place + 128 * (block % 2) < lengths_ref[block // 2]
            peak = jnp.maximum(peak, jnp.where(valid, jnp.abs(normed), 0.0))
        page_ref[0, tile : tile + 1, :] = jnp.max(peak, axis=0, keepdims=True)
    page_ref[0, 12:15, :] = jnp.max(sums_ref[:, 8:11, :], axis=0)
    page_ref[0, 15:16, :] = jnp.zeros((1, 128), jnp.float32)
    page = page_ref[0]
    for peer in range(1, page_ref.shape[0]):
        page_ref[peer] = page


def peak_kernel(place_ref, maxima_ref, sums_ref, acts_ref, gain_ref, bias_ref, page_ref):
    columns = moments(sums_ref[...])
    act = jnp.max(maxima_ref[:, 0:12, :], axis=0)
    start = 8 * place_ref[1]
    for pair in range(4):
        both = jnp.maximum(maxima_ref[start + 2 * pair, 12:15, :], maxima_ref[start + 2 * pair + 1, 12:15, :])
        page_ref[0, 3 * pair : 3 * pair + 3, :] = both
    scale = jnp.sqrt(act + EPS) / jnp.sqrt(page_ref[0, 0:12, :] + EPS)
    page_ref[0, 0:12, :] = scale
    inverse = 1.0 / scale
    for block in range(4):
        peak = jnp.zeros((128, 128), jnp.float32)
        for tile in range(12):
            x = acts_ref[pl.ds(128 * block, 128), pl.ds(128 * tile, 128)].astype(jnp.float32)
            gain = gain_ref[tile : tile + 1, :]
            bias = bias_ref[tile : tile + 1, :]
            normed = (x - columns[:, block : block + 1]) * columns[:, 4 + block : 5 + block] * gain + bias
            peak = jnp.maximum(peak, jnp.abs(normed) * inverse[tile : tile + 1])
        page_ref[0, 12 + block : 13 + block, :] = jnp.max(peak.T, axis=0, keepdims=True)
    page = page_ref[0]
    for peer in range(1, page_ref.shape[0]):
        page_ref[peer] = page


def serve_kernel(place_ref, lengths_ref, blocks_ref, pages_ref, served_ref, scale_ref, tok_ref):
    scale_ref[...] = blocks_ref[place_ref[1], 0:12, :]
    peaks = jnp.max(blocks_ref[:, 12:16, :], axis=0)
    lane = lax.broadcasted_iota(jnp.int32, (1, 128), 1)
    for block in range(4):
        valid = lane + 128 * (block % 2) < lengths_ref[block // 2]
        tok_ref[block : block + 1, :] = jnp.where(valid, peaks[block : block + 1], 0.0)
    low = lax.broadcasted_iota(jnp.int32, (24, 128), 1) < 64
    for pair in range(32):
        even = pages_ref[2 * pair].astype(jnp.float32)
        odd = pages_ref[2 * pair + 1].astype(jnp.float32)
        upper = jnp.where(low, even[48:72], odd[48:72])
        lower = pltpu.roll(jnp.where(low, odd[48:72], even[48:72]), 64, 1)
        middle = jnp.concatenate([upper, lower], axis=0)
        for part, tile in enumerate((even[0:48], middle, odd[0:48])):
            row = 3 * pair + part
            scale = blocks_ref[row // 12, row % 12 : row % 12 + 1, :]
            served_ref[:, pl.ds(128 * row, 128)] = (tile * scale).astype(jnp.bfloat16)


def body(acts, lengths, ln_gain, ln_bias, w_fc1):
    place = jnp.stack([lax.axis_index("dp"), lax.axis_index("mp")]).astype(jnp.int32)
    gain = ln_gain.reshape(12, 128)
    bias = ln_bias.reshape(12, 128)
    with jax.named_scope("token_moments"):
        page = pl.pallas_call(
            stats_kernel,
            out_shape=jax.ShapeDtypeStruct((8, 16, 128), jnp.float32),
            in_specs=[SMEM_SPEC, VMEM_SPEC, VMEM_SPEC],
            out_specs=VMEM_SPEC,
            scratch_shapes=[pltpu.VMEM((384, 128), jnp.float32)],
            compiler_params=params(),
        )(place, acts, w_fc1)
        sums = lax.all_to_all(page, "mp", 0, 0, tiled=True)
    with jax.named_scope("weight_exchange"):
        packed = pl.pallas_call(
            pack_kernel,
            out_shape=jax.ShapeDtypeStruct((64, 72, 128), jnp.bfloat16),
            in_specs=[SMEM_SPEC, VMEM_SPEC],
            out_specs=VMEM_SPEC,
            compiler_params=params(),
        )(place, w_fc1)
        pages = lax.all_to_all(packed, "dp", 0, 0, tiled=True)
    with jax.named_scope("channel_maxima"):
        page = pl.pallas_call(
            act_kernel,
            out_shape=jax.ShapeDtypeStruct((64, 16, 128), jnp.float32),
            in_specs=[SMEM_SPEC] + [VMEM_SPEC] * 4,
            out_specs=VMEM_SPEC,
            compiler_params=params(),
        )(lengths, sums, acts, gain, bias)
        maxima = lax.all_to_all(page, "dp", 0, 0, tiled=True)
    with jax.named_scope("token_peaks"):
        page = pl.pallas_call(
            peak_kernel,
            out_shape=jax.ShapeDtypeStruct((8, 16, 128), jnp.float32),
            in_specs=[SMEM_SPEC] + [VMEM_SPEC] * 5,
            out_specs=VMEM_SPEC,
            compiler_params=params(),
        )(place, maxima, sums, acts, gain, bias)
        blocks = lax.all_to_all(page, "mp", 0, 0, tiled=True)
    with jax.named_scope("smoothed_weight"):
        served, scale, tok = pl.pallas_call(
            serve_kernel,
            out_shape=(
                jax.ShapeDtypeStruct((48, D), jnp.bfloat16),
                jax.ShapeDtypeStruct((12, 128), jnp.float32),
                jax.ShapeDtypeStruct((4, 128), jnp.float32),
            ),
            in_specs=[SMEM_SPEC, SMEM_SPEC, VMEM_SPEC, VMEM_SPEC],
            out_specs=(VMEM_SPEC,) * 3,
            compiler_params=params(),
        )(place, lengths, blocks, pages)
    return served, scale.reshape(1536), tok.reshape(512)


def solution(mesh):
    return jax.shard_map(
        body,
        mesh=mesh,
        in_specs=(P("dp", "mp"), P("dp"), P("mp"), P("mp"), P("dp", "mp")),
        out_specs=(P(("mp", "dp"), None), P("mp"), P("dp")),
        check_vma=False,
    )
```

```python
import jax
import jax.numpy as jnp
from jax import lax
from jax.experimental import pallas as pl
from jax.experimental.pallas import tpu as pltpu
from jax.sharding import PartitionSpec as P

D = 12288
SLOT = 256
EPS = 1e-05
VMEM_SPEC = pl.BlockSpec(memory_space=pltpu.VMEM)
SMEM_SPEC = pl.BlockSpec(memory_space=pltpu.SMEM)


def params():
    return pltpu.CompilerParams(vmem_limit_bytes=40 * 1024 * 1024)


def stats_kernel(place_ref, acts_ref, w_ref, page_ref, rows_ref):
    parity = place_ref[0] % 2
    for block in range(4):
        total = jnp.zeros((128, 128), jnp.float32)
        square = jnp.zeros((128, 128), jnp.float32)
        for tile in range(12):
            x = acts_ref[pl.ds(128 * block, 128), pl.ds(128 * tile, 128)].astype(jnp.float32)
            total = total + x
            square = square + x * x
        page_ref[block : block + 1, :] = jnp.sum(total.T, axis=0, keepdims=True)
        page_ref[4 + block : 5 + block, :] = jnp.sum(square.T, axis=0, keepdims=True)
    rows_ref[...] = jnp.zeros_like(rows_ref)
    for part in range(2):
        peak = jnp.zeros((96, 128), jnp.float32)
        for tile in range(24):
            peak = jnp.maximum(peak, jnp.abs(w_ref[pl.ds(96 * part, 96), pl.ds(128 * tile, 128)].astype(jnp.float32)))
        rows_ref[pl.ds(pl.multiple_of(192 * parity + 96 * part, 32), 96), :] = peak
    for block in range(3):
        page_ref[8 + block : 9 + block, :] = jnp.max(rows_ref[pl.ds(128 * block, 128), :].T, axis=0, keepdims=True)
    page_ref[11:16, :] = jnp.zeros((5, 128), jnp.float32)


def pack_kernel(place_ref, w_ref, page_ref):
    parity = place_ref[0] % 2
    low = lax.broadcasted_iota(jnp.int32, (24, 128), 1) < 64
    first = low == (parity == 0)

    def step(index, carry):
        columns = pl.ds(pl.multiple_of(384 * index, 128), 384)
        full = w_ref[pl.ds(pl.multiple_of(64 * parity, 64), 128), columns].astype(jnp.float32).T
        half = w_ref[pl.ds(pl.multiple_of(128 * (1 - parity), 64), 64), columns].astype(jnp.float32)
        twice = jnp.concatenate([half, half], axis=0).T
        for peer in range(8):
            upper = twice[48 * peer : 48 * peer + 24]
            lower = twice[48 * peer + 24 : 48 * peer + 48]
            page = jnp.concatenate([full[48 * peer : 48 * peer + 48], jnp.where(first, upper, lower)], axis=0)
            page_ref[8 * index + peer] = page.astype(jnp.bfloat16)
        return carry

    lax.fori_loop(0, 8, step, 0)


def moments(sums):
    mean = sums[0:4] / D
    var = sums[4:8] / D - mean * mean
    rstd = lax.rsqrt(var + EPS)
    return jnp.concatenate([mean, rstd], axis=0).T


def act_kernel(place_ref, lengths_ref, sums_ref, acts_ref, gain_ref, bias_ref, page_ref):
    columns = moments(sums_ref[...])
    place = lax.broadcasted_iota(jnp.int32, (128, 1), 0)
    for tile in range(12):
        gain = gain_ref[tile : tile + 1, :]
        bias = bias_ref[tile : tile + 1, :]
        peak = jnp.zeros((128, 128), jnp.float32)
        for block in range(4):
            x = acts_ref[pl.ds(128 * block, 128), pl.ds(128 * tile, 128)].astype(jnp.float32)
            normed = (x - columns[:, block : block + 1]) * columns[:, 4 + block : 5 + block] * gain + bias
            valid = place + 128 * (block % 2) < lengths_ref[block // 2]
            peak = jnp.maximum(peak, jnp.where(valid, jnp.abs(normed), 0.0))
        page_ref[tile : tile + 1, :] = jnp.max(peak, axis=0, keepdims=True)
    pair = (place_ref[0] // 2) % 4
    for slot in range(4):
        page_ref[12 + 3 * slot : 15 + 3 * slot, :] = jnp.where(pair == slot, sums_ref[8:11, :], 0.0)


def peak_kernel(pages_ref, maxima_ref, sums_ref, acts_ref, gain_ref, bias_ref, page_ref):
    del pages_ref
    columns = moments(sums_ref[...])
    scale = jnp.sqrt(maxima_ref[0:12, :] + EPS) / jnp.sqrt(maxima_ref[12:24, :] + EPS)
    page_ref[0, 0:12, :] = scale
    inverse = 1.0 / scale
    for block in range(4):
        peak = jnp.zeros((128, 128), jnp.float32)
        for tile in range(12):
            x = acts_ref[pl.ds(128 * block, 128), pl.ds(128 * tile, 128)].astype(jnp.float32)
            gain = gain_ref[tile : tile + 1, :]
            bias = bias_ref[tile : tile + 1, :]
            normed = (x - columns[:, block : block + 1]) * columns[:, 4 + block : 5 + block] * gain + bias
            peak = jnp.maximum(peak, jnp.abs(normed) * inverse[tile : tile + 1])
        page_ref[0, 12 + block : 13 + block, :] = jnp.max(peak.T, axis=0, keepdims=True)
    page = page_ref[0]
    for peer in range(1, page_ref.shape[0]):
        page_ref[peer] = page


def serve_kernel(place_ref, lengths_ref, blocks_ref, pages_ref, served_ref, scale_ref, tok_ref):
    scale_ref[...] = blocks_ref[place_ref[1], 0:12, :]
    peaks = jnp.max(blocks_ref[:, 12:16, :], axis=0)
    lane = lax.broadcasted_iota(jnp.int32, (1, 128), 1)
    for block in range(4):
        valid = lane + 128 * (block % 2) < lengths_ref[block // 2]
        tok_ref[block : block + 1, :] = jnp.where(valid, peaks[block : block + 1], 0.0)
    low = lax.broadcasted_iota(jnp.int32, (24, 128), 1) < 64
    for pair in range(32):
        even = pages_ref[2 * pair].astype(jnp.float32)
        odd = pages_ref[2 * pair + 1].astype(jnp.float32)
        upper = jnp.where(low, even[48:72], odd[48:72])
        lower = pltpu.roll(jnp.where(low, odd[48:72], even[48:72]), 64, 1)
        middle = jnp.concatenate([upper, lower], axis=0)
        for part, tile in enumerate((even[0:48], middle, odd[0:48])):
            row = 3 * pair + part
            scale = blocks_ref[row // 12, row % 12 : row % 12 + 1, :]
            served_ref[:, pl.ds(128 * row, 128)] = (tile * scale).astype(jnp.bfloat16)


def swap(x, axis, bit):
    size = lax.axis_size(axis)
    return lax.ppermute(x, axis, [(i, i ^ bit) for i in range(size)])


def body(acts, lengths, ln_gain, ln_bias, w_fc1):
    dp_place = lax.axis_index("dp")
    mp_place = lax.axis_index("mp")
    place = jnp.stack([dp_place, mp_place]).astype(jnp.int32)
    gain = ln_gain.reshape(12, 128)
    bias = ln_bias.reshape(12, 128)
    with jax.named_scope("weight_exchange"):
        packed = pl.pallas_call(
            pack_kernel,
            out_shape=jax.ShapeDtypeStruct((64, 72, 128), jnp.bfloat16),
            in_specs=[SMEM_SPEC, VMEM_SPEC],
            out_specs=VMEM_SPEC,
            compiler_params=params(),
        )(place, w_fc1)
        pages = lax.all_to_all(packed, "dp", 0, 0, tiled=True)
    with jax.named_scope("token_moments"):
        sums = pl.pallas_call(
            stats_kernel,
            out_shape=jax.ShapeDtypeStruct((16, 128), jnp.float32),
            in_specs=[SMEM_SPEC, VMEM_SPEC, VMEM_SPEC],
            out_specs=VMEM_SPEC,
            scratch_shapes=[pltpu.VMEM((384, 128), jnp.float32)],
            compiler_params=params(),
        )(place, acts, w_fc1)
        added = lax.broadcasted_iota(jnp.int32, (16, 128), 0) < 8
        for bit in (1, 2, 4):
            other = swap(sums, "mp", bit)
            sums = jnp.where(added, sums + other, jnp.maximum(sums, other))
    with jax.named_scope("channel_maxima"):
        maxima = pl.pallas_call(
            act_kernel,
            out_shape=jax.ShapeDtypeStruct((24, 128), jnp.float32),
            in_specs=[SMEM_SPEC] * 2 + [VMEM_SPEC] * 4,
            out_specs=VMEM_SPEC,
            compiler_params=params(),
        )(place, lengths, sums, acts, gain, bias)
        for bit in (1, 2, 4):
            maxima = jnp.maximum(maxima, swap(maxima, "dp", bit))
        kept = (lax.broadcasted_iota(jnp.int32, (24, 128), 0) < 12) | (dp_place // 8 == mp_place)
        maxima = jnp.where(kept, maxima, 0.0)
        for bit in (8, 16, 32):
            maxima = jnp.maximum(maxima, swap(maxima, "dp", bit))
    with jax.named_scope("token_peaks"):
        page = pl.pallas_call(
            peak_kernel,
            out_shape=jax.ShapeDtypeStruct((8, 16, 128), jnp.float32),
            in_specs=[pl.BlockSpec(memory_space=pl.ANY)] + [VMEM_SPEC] * 5,
            out_specs=VMEM_SPEC,
            compiler_params=params(),
        )(pages, maxima, sums, acts, gain, bias)
        blocks = lax.all_to_all(page, "mp", 0, 0, tiled=True)
    with jax.named_scope("smoothed_weight"):
        served, scale, tok = pl.pallas_call(
            serve_kernel,
            out_shape=(
                jax.ShapeDtypeStruct((48, D), jnp.bfloat16),
                jax.ShapeDtypeStruct((12, 128), jnp.float32),
                jax.ShapeDtypeStruct((4, 128), jnp.float32),
            ),
            in_specs=[SMEM_SPEC, SMEM_SPEC, VMEM_SPEC, VMEM_SPEC],
            out_specs=(VMEM_SPEC,) * 3,
            compiler_params=params(),
        )(place, lengths, blocks, pages)
    return served, scale.reshape(1536), tok.reshape(512)


def solution(mesh):
    return jax.shard_map(
        body,
        mesh=mesh,
        in_specs=(P("dp", "mp"), P("dp"), P("mp"), P("mp"), P("dp", "mp")),
        out_specs=(P(("mp", "dp"), None), P("mp"), P("dp")),
        check_vma=False,
    )
```

```python
import jax
import jax.numpy as jnp
from jax import lax
from jax.experimental import pallas as pl
from jax.experimental.pallas import tpu as pltpu
from jax.sharding import PartitionSpec as P

D = 12288
SLOT = 256
EPS = 1e-05
VMEM_SPEC = pl.BlockSpec(memory_space=pltpu.VMEM)
SMEM_SPEC = pl.BlockSpec(memory_space=pltpu.SMEM)


def params(mebibytes=40):
    return pltpu.CompilerParams(vmem_limit_bytes=mebibytes * 1024 * 1024)


def pack_kernel(place_ref, w_ref, page_ref, peak_ref, rows_ref):
    step = pl.program_id(0)
    parity = place_ref[0] % 2
    low = lax.broadcasted_iota(jnp.int32, (24, 128), 1) < 64
    first = low == (parity == 0)

    @pl.when(step == 0)
    def _():
        rows_ref[...] = jnp.zeros_like(rows_ref)

    own = pl.ds(pl.multiple_of(192 * parity, 64), 192)
    w = jnp.abs(w_ref[...].astype(jnp.float32))
    peak = jnp.maximum(jnp.maximum(w[:, 0:128], w[:, 128:256]), w[:, 256:384])
    rows_ref[own, :] = jnp.maximum(rows_ref[own, :], peak)
    full = w_ref[pl.ds(pl.multiple_of(64 * parity, 64), 128), :].astype(jnp.float32).T
    half = w_ref[pl.ds(pl.multiple_of(128 * (1 - parity), 64), 64), :].astype(jnp.float32)
    twice = jnp.concatenate([half, half], axis=0).T
    for peer in range(8):
        upper = twice[48 * peer : 48 * peer + 24]
        lower = twice[48 * peer + 24 : 48 * peer + 48]
        page = jnp.concatenate([full[48 * peer : 48 * peer + 48], jnp.where(first, upper, lower)], axis=0)
        page_ref[peer] = page.astype(jnp.bfloat16)

    @pl.when(step == pl.num_programs(0) - 1)
    def _():
        for block in range(3):
            peak_ref[block : block + 1, :] = jnp.max(rows_ref[pl.ds(128 * block, 128), :].T, axis=0, keepdims=True)
        peak_ref[3:8, :] = jnp.zeros((5, 128), jnp.float32)


def stats_kernel(peak_ref, acts_ref, page_ref):
    page_ref[8:16, :] = peak_ref[...]
    for block in range(4):
        total = jnp.zeros((128, 128), jnp.float32)
        square = jnp.zeros((128, 128), jnp.float32)
        for tile in range(12):
            x = acts_ref[pl.ds(128 * block, 128), pl.ds(128 * tile, 128)].astype(jnp.float32)
            total = total + x
            square = square + x * x
        page_ref[block : block + 1, :] = jnp.sum(total.T, axis=0, keepdims=True)
        page_ref[4 + block : 5 + block, :] = jnp.sum(square.T, axis=0, keepdims=True)


def moments(sums):
    mean = sums[0:4] / D
    var = sums[4:8] / D - mean * mean
    rstd = lax.rsqrt(var + EPS)
    return jnp.concatenate([mean, rstd], axis=0).T


def act_kernel(lengths_ref, sums_ref, acts_ref, gain_ref, bias_ref, page_ref):
    columns = moments(sums_ref[...])
    place = lax.broadcasted_iota(jnp.int32, (128, 1), 0)
    for tile in range(12):
        gain = gain_ref[tile : tile + 1, :]
        bias = bias_ref[tile : tile + 1, :]
        peak = jnp.zeros((128, 128), jnp.float32)
        for block in range(4):
            x = acts_ref[pl.ds(128 * block, 128), pl.ds(128 * tile, 128)].astype(jnp.float32)
            normed = (x - columns[:, block : block + 1]) * columns[:, 4 + block : 5 + block] * gain + bias
            valid = place + 128 * (block % 2) < lengths_ref[block // 2]
            peak = jnp.maximum(peak, jnp.where(valid, jnp.abs(normed), 0.0))
        page_ref[tile : tile + 1, :] = jnp.max(peak, axis=0, keepdims=True)
    page_ref[12:15, :] = sums_ref[8:11, :]
    page_ref[15:16, :] = jnp.zeros((1, 128), jnp.float32)


def peak_kernel(place_ref, maxima_ref, sums_ref, acts_ref, gain_ref, bias_ref, page_ref):
    columns = moments(sums_ref[...])
    act = jnp.max(maxima_ref[:, 0:12, :], axis=0)
    for slot in range(4):
        page_ref[0, 3 * slot : 3 * slot + 3, :] = maxima_ref[4 * place_ref[1] + slot, 12:15, :]
    scale = jnp.sqrt(act + EPS) / jnp.sqrt(page_ref[0, 0:12, :] + EPS)
    page_ref[0, 0:12, :] = scale
    inverse = 1.0 / scale
    for block in range(4):
        peak = jnp.zeros((128, 128), jnp.float32)
        for tile in range(12):
            x = acts_ref[pl.ds(128 * block, 128), pl.ds(128 * tile, 128)].astype(jnp.float32)
            gain = gain_ref[tile : tile + 1, :]
            bias = bias_ref[tile : tile + 1, :]
            normed = (x - columns[:, block : block + 1]) * columns[:, 4 + block : 5 + block] * gain + bias
            peak = jnp.maximum(peak, jnp.abs(normed) * inverse[tile : tile + 1])
        page_ref[0, 12 + block : 13 + block, :] = jnp.max(peak.T, axis=0, keepdims=True)
    page = page_ref[0]
    for peer in range(1, page_ref.shape[0]):
        page_ref[peer] = page


def serve_kernel(place_ref, lengths_ref, blocks_ref, pages_ref, served_ref, scale_ref, tok_ref):
    step = pl.program_id(0)

    @pl.when(step == 0)
    def _():
        scale_ref[...] = blocks_ref[place_ref[1], 0:12, :]
        peaks = jnp.max(blocks_ref[:, 12:16, :], axis=0)
        lane = lax.broadcasted_iota(jnp.int32, (1, 128), 1)
        for block in range(4):
            valid = lane + 128 * (block % 2) < lengths_ref[block // 2]
            tok_ref[block : block + 1, :] = jnp.where(valid, peaks[block : block + 1], 0.0)

    low = lax.broadcasted_iota(jnp.int32, (24, 128), 1) < 64
    for pair in range(8):
        even = pages_ref[2 * pair].astype(jnp.float32)
        odd = pages_ref[2 * pair + 1].astype(jnp.float32)
        upper = jnp.where(low, even[48:72], odd[48:72])
        lower = pltpu.roll(jnp.where(low, odd[48:72], even[48:72]), 64, 1)
        middle = jnp.concatenate([upper, lower], axis=0)
        for part, tile in enumerate((even[0:48], middle, odd[0:48])):
            row = 3 * pair + part
            scale = blocks_ref[2 * step + row // 12, row % 12 : row % 12 + 1, :]
            served_ref[:, pl.ds(128 * row, 128)] = (tile * scale).astype(jnp.bfloat16)


def swap(x, axis, bit):
    size = lax.axis_size(axis)
    return lax.ppermute(x, axis, [(i, i ^ bit) for i in range(size)])


def body(acts, lengths, ln_gain, ln_bias, w_fc1):
    dp_place = lax.axis_index("dp")
    mp_place = lax.axis_index("mp")
    place = jnp.stack([dp_place, mp_place]).astype(jnp.int32)
    gain = ln_gain.reshape(12, 128)
    bias = ln_bias.reshape(12, 128)
    whole = lambda *shape: pl.BlockSpec(shape, lambda step: (0,) * len(shape))
    with jax.named_scope("weight_exchange"):
        packed, w_peak = pl.pallas_call(
            pack_kernel,
            grid=(8,),
            out_shape=(
                jax.ShapeDtypeStruct((64, 72, 128), jnp.bfloat16),
                jax.ShapeDtypeStruct((8, 128), jnp.float32),
            ),
            in_specs=[SMEM_SPEC, pl.BlockSpec((192, 384), lambda step: (0, step))],
            out_specs=(pl.BlockSpec((8, 72, 128), lambda step: (step, 0, 0)), whole(8, 128)),
            scratch_shapes=[pltpu.VMEM((384, 128), jnp.float32)],
            compiler_params=params(60),
        )(place, w_fc1)
        pages = lax.all_to_all(packed, "dp", 0, 0, tiled=True)
    with jax.named_scope("token_moments"):
        sums = pl.pallas_call(
            stats_kernel,
            out_shape=jax.ShapeDtypeStruct((16, 128), jnp.float32),
            in_specs=[VMEM_SPEC, VMEM_SPEC],
            out_specs=VMEM_SPEC,
            compiler_params=params(),
        )(w_peak, acts)
        added = lax.broadcasted_iota(jnp.int32, (16, 128), 0) < 8
        for bit in (1, 2, 4):
            other = swap(sums, "mp", bit)
            sums = jnp.where(added, sums + other, jnp.maximum(sums, other))
    with jax.named_scope("channel_maxima"):
        maxima = pl.pallas_call(
            act_kernel,
            out_shape=jax.ShapeDtypeStruct((16, 128), jnp.float32),
            in_specs=[SMEM_SPEC] + [VMEM_SPEC] * 4,
            out_specs=VMEM_SPEC,
            compiler_params=params(),
        )(lengths, sums, acts, gain, bias)
        maxima = jnp.maximum(maxima, swap(maxima, "dp", 1))
        maxima, pages = lax.optimization_barrier((maxima, pages))
        copies = jnp.broadcast_to(maxima[None], (32, 16, 128))
        kinds = [[2 * chip + core for chip in range(32)] for core in range(2)]
        maxima = lax.all_to_all(copies, "dp", 0, 0, axis_index_groups=kinds, tiled=True)
    with jax.named_scope("token_peaks"):
        page = pl.pallas_call(
            peak_kernel,
            out_shape=jax.ShapeDtypeStruct((8, 16, 128), jnp.float32),
            in_specs=[SMEM_SPEC] + [VMEM_SPEC] * 5,
            out_specs=VMEM_SPEC,
            compiler_params=params(),
        )(place, maxima, sums, acts, gain, bias)
        blocks = lax.all_to_all(page, "mp", 0, 0, tiled=True)
    with jax.named_scope("smoothed_weight"):
        served, scale, tok = pl.pallas_call(
            serve_kernel,
            grid=(4,),
            out_shape=(
                jax.ShapeDtypeStruct((48, D), jnp.bfloat16),
                jax.ShapeDtypeStruct((12, 128), jnp.float32),
                jax.ShapeDtypeStruct((4, 128), jnp.float32),
            ),
            in_specs=[SMEM_SPEC, SMEM_SPEC, whole(8, 16, 128), pl.BlockSpec((16, 72, 128), lambda step: (step, 0, 0))],
            out_specs=(pl.BlockSpec((48, 3072), lambda step: (0, step)), whole(12, 128), whole(4, 128)),
            compiler_params=params(),
        )(place, lengths, blocks, pages)
    return served, scale.reshape(1536), tok.reshape(512)


def solution(mesh):
    return jax.shard_map(
        body,
        mesh=mesh,
        in_specs=(P("dp", "mp"), P("dp"), P("mp"), P("mp"), P("dp", "mp")),
        out_specs=(P(("mp", "dp"), None), P("mp"), P("dp")),
        check_vma=False,
    )
```

```python
import jax
import jax.numpy as jnp
from jax import lax
from jax.experimental import pallas as pl
from jax.experimental.pallas import tpu as pltpu
from jax.sharding import PartitionSpec as P

D = 12288
SLOT = 256
EPS = 1e-05
VMEM_SPEC = pl.BlockSpec(memory_space=pltpu.VMEM)
SMEM_SPEC = pl.BlockSpec(memory_space=pltpu.SMEM)
ANY_SPEC = pl.BlockSpec(memory_space=pl.ANY)


def params(mebibytes=40):
    return pltpu.CompilerParams(vmem_limit_bytes=mebibytes * 1024 * 1024)


def pack_kernel(w_hbm, page_hbm, peak_ref, w_ref, page_ref, rows_ref, in_sems, out_sems):
    parity = lax.axis_index("dp") % 2
    low = lax.broadcasted_iota(jnp.int32, (24, 128), 1) < 64
    first = low == (parity == 0)
    own = pl.ds(pl.multiple_of(192 * parity, 64), 192)

    def columns(step):
        return pl.ds(pl.multiple_of(384 * step, 128), 384)

    def fetch(step):
        return pltpu.make_async_copy(w_hbm.at[:, columns(step)], w_ref.at[:, columns(step)], in_sems.at[step])

    def store(step):
        peers = pl.ds(8 * step, 8)
        return pltpu.make_async_copy(page_ref.at[peers], page_hbm.at[peers], out_sems.at[step])

    for step in range(8):
        fetch(step).start()
    rows_ref[...] = jnp.zeros_like(rows_ref)

    def pack(step, carry):
        fetch(step).wait()
        w = jnp.abs(w_ref[:, columns(step)].astype(jnp.float32))
        peak = jnp.maximum(jnp.maximum(w[:, 0:128], w[:, 128:256]), w[:, 256:384])
        rows_ref[own, :] = jnp.maximum(rows_ref[own, :], peak)
        full = w_ref[pl.ds(pl.multiple_of(64 * parity, 64), 128), columns(step)].astype(jnp.float32).T
        half = w_ref[pl.ds(pl.multiple_of(128 * (1 - parity), 64), 64), columns(step)].astype(jnp.float32)
        twice = jnp.concatenate([half, half], axis=0).T
        for peer in range(8):
            upper = twice[48 * peer : 48 * peer + 24]
            lower = twice[48 * peer + 24 : 48 * peer + 48]
            page = jnp.concatenate([full[48 * peer : 48 * peer + 48], jnp.where(first, upper, lower)], axis=0)
            page_ref[8 * step + peer] = page.astype(jnp.bfloat16)
        store(step).start()
        return carry

    lax.fori_loop(0, 8, pack, 0)
    for block in range(3):
        peak_ref[block : block + 1, :] = jnp.max(rows_ref[pl.ds(128 * block, 128), :].T, axis=0, keepdims=True)
    peak_ref[3:8, :] = jnp.zeros((5, 128), jnp.float32)
    for step in range(8):
        store(step).wait()


def stats_kernel(peak_ref, acts_ref, page_ref):
    page_ref[8:16, :] = peak_ref[...]
    for block in range(4):
        total = jnp.zeros((128, 128), jnp.float32)
        square = jnp.zeros((128, 128), jnp.float32)
        for tile in range(12):
            x = acts_ref[pl.ds(128 * block, 128), pl.ds(128 * tile, 128)].astype(jnp.float32)
            total = total + x
            square = square + x * x
        page_ref[block : block + 1, :] = jnp.sum(total.T, axis=0, keepdims=True)
        page_ref[4 + block : 5 + block, :] = jnp.sum(square.T, axis=0, keepdims=True)


def moments(sums):
    mean = sums[0:4] / D
    var = sums[4:8] / D - mean * mean
    rstd = lax.rsqrt(var + EPS)
    return jnp.concatenate([mean, rstd], axis=0).T


def act_kernel(lengths_ref, sums_ref, acts_ref, gain_ref, bias_ref, page_ref):
    columns = moments(sums_ref[...])
    place = lax.broadcasted_iota(jnp.int32, (128, 128), 0)
    peaks = [jnp.zeros((8, 128), jnp.float32)] * 12
    for block in range(4):
        mean = jnp.broadcast_to(columns[:, block : block + 1], (128, 128))
        rstd = jnp.broadcast_to(columns[:, 4 + block : 5 + block], (128, 128))
        valid = place + 128 * (block % 2) < lengths_ref[block // 2]
        for tile in range(12):
            x = acts_ref[pl.ds(128 * block, 128), pl.ds(128 * tile, 128)].astype(jnp.float32)
            normed = (x - mean) * rstd * gain_ref[tile : tile + 1, :] + bias_ref[tile : tile + 1, :]
            peak = jnp.where(valid, jnp.abs(normed), 0.0)
            peaks[tile] = jnp.maximum(peaks[tile], jnp.max(peak.reshape(16, 8, 128), axis=0))
    for tile in range(12):
        page_ref[tile : tile + 1, :] = jnp.max(peaks[tile], axis=0, keepdims=True)
    kept = lax.axis_index("dp") // 8 == lax.axis_index("mp")
    page_ref[12:15, :] = jnp.where(kept, sums_ref[8:11, :], 0.0)
    page_ref[15:16, :] = jnp.zeros((1, 128), jnp.float32)


def peak_kernel(maxima_ref, sums_ref, acts_ref, gain_ref, bias_ref, page_ref):
    columns = moments(sums_ref[...])
    start = 4 * (lax.axis_index("mp") // 2)
    act = jnp.max(maxima_ref[:, 0:12, :], axis=0)
    for slot in range(4):
        page_ref[0, 3 * slot : 3 * slot + 3, :] = maxima_ref[start + slot, 12:15, :]
    scale = jnp.sqrt(act + EPS) / jnp.sqrt(page_ref[0, 0:12, :] + EPS)
    page_ref[0, 0:12, :] = scale
    inverse = 1.0 / scale
    gain = gain_ref[...] * inverse
    bias = bias_ref[...] * inverse
    for block in range(4):
        mean = jnp.broadcast_to(columns[:, block : block + 1], (128, 128))
        rstd = jnp.broadcast_to(columns[:, 4 + block : 5 + block], (128, 128))
        peak = jnp.zeros((128, 128), jnp.float32)
        for tile in range(12):
            x = acts_ref[pl.ds(128 * block, 128), pl.ds(128 * tile, 128)].astype(jnp.float32)
            smoothed = (x - mean) * rstd * gain[tile : tile + 1] + bias[tile : tile + 1]
            peak = jnp.maximum(peak, jnp.abs(smoothed))
        page_ref[0, 12 + block : 13 + block, :] = jnp.max(peak.T, axis=0, keepdims=True)
    page = page_ref[0]
    for peer in range(1, page_ref.shape[0]):
        page_ref[peer] = page


def serve_kernel(lengths_ref, blocks_ref, pages_ref, served_hbm, scale_ref, tok_ref, served_ref, sems):
    low = lax.broadcasted_iota(jnp.int32, (24, 128), 1) < 64

    def store(step):
        columns = pl.ds(pl.multiple_of(3072 * step, 128), 3072)
        return pltpu.make_async_copy(served_ref.at[:, columns], served_hbm.at[:, columns], sems.at[step])

    for step in range(4):
        for pair in range(8 * step, 8 * step + 8):
            even = pages_ref[2 * pair].astype(jnp.float32)
            odd = pages_ref[2 * pair + 1].astype(jnp.float32)
            upper = jnp.where(low, even[48:72], odd[48:72])
            lower = pltpu.roll(jnp.where(low, odd[48:72], even[48:72]), 64, 1)
            middle = jnp.concatenate([upper, lower], axis=0)
            for part, tile in enumerate((even[0:48], middle, odd[0:48])):
                row = 3 * pair + part
                scale = blocks_ref[row // 12, row % 12 : row % 12 + 1, :]
                served_ref[:, pl.ds(128 * row, 128)] = (tile * scale).astype(jnp.bfloat16)
        store(step).start()
    scale_ref[...] = blocks_ref[lax.axis_index("mp"), 0:12, :]
    peaks = jnp.max(blocks_ref[:, 12:16, :], axis=0)
    lane = lax.broadcasted_iota(jnp.int32, (1, 128), 1)
    for block in range(4):
        valid = lane + 128 * (block % 2) < lengths_ref[block // 2]
        tok_ref[block : block + 1, :] = jnp.where(valid, peaks[block : block + 1], 0.0)
    for step in range(4):
        store(step).wait()


def swap(x, axis, bit):
    size = lax.axis_size(axis)
    return lax.ppermute(x, axis, [(i, i ^ bit) for i in range(size)])


def body(acts, lengths, ln_gain, ln_bias, w_fc1):
    gain = ln_gain.reshape(12, 128)
    bias = ln_bias.reshape(12, 128)
    with jax.named_scope("weight_exchange"):
        packed, w_peak = pl.pallas_call(
            pack_kernel,
            out_shape=(
                jax.ShapeDtypeStruct((64, 72, 128), jnp.bfloat16),
                jax.ShapeDtypeStruct((8, 128), jnp.float32),
            ),
            in_specs=[ANY_SPEC],
            out_specs=(ANY_SPEC, VMEM_SPEC),
            scratch_shapes=[
                pltpu.VMEM((192, 3072), jnp.bfloat16),
                pltpu.VMEM((64, 72, 128), jnp.bfloat16),
                pltpu.VMEM((384, 128), jnp.float32),
                pltpu.SemaphoreType.DMA((8,)),
                pltpu.SemaphoreType.DMA((8,)),
            ],
            compiler_params=params(60),
        )(w_fc1)
        pages = lax.all_to_all(packed, "dp", 0, 0, tiled=True)
    with jax.named_scope("token_moments"):
        sums = pl.pallas_call(
            stats_kernel,
            out_shape=jax.ShapeDtypeStruct((16, 128), jnp.float32),
            in_specs=[VMEM_SPEC, VMEM_SPEC],
            out_specs=VMEM_SPEC,
            compiler_params=params(),
        )(w_peak, acts)
        added = lax.broadcasted_iota(jnp.int32, (16, 128), 0) < 8
        for bit in (1, 2, 4):
            other = swap(sums, "mp", bit)
            sums = jnp.where(added, sums + other, jnp.maximum(sums, other))
    with jax.named_scope("channel_maxima"):
        maxima = pl.pallas_call(
            act_kernel,
            out_shape=jax.ShapeDtypeStruct((16, 128), jnp.float32),
            in_specs=[SMEM_SPEC] + [VMEM_SPEC] * 4,
            out_specs=VMEM_SPEC,
            compiler_params=params(),
        )(lengths, sums, acts, gain, bias)
        for bit in (1, 8):
            maxima = jnp.maximum(maxima, swap(maxima, "dp", bit))
        maxima, pages = lax.optimization_barrier((maxima, pages))
        copies = jnp.broadcast_to(maxima[None], (16, 16, 128))
        kinds = [[16 * pair + 8 * plane + 2 * y + core for pair in range(4) for y in range(4)] for plane in (0, 1) for core in (0, 1)]
        maxima = lax.all_to_all(copies, "dp", 0, 0, axis_index_groups=kinds, tiled=True)
    with jax.named_scope("token_peaks"):
        page = pl.pallas_call(
            peak_kernel,
            out_shape=jax.ShapeDtypeStruct((8, 16, 128), jnp.float32),
            in_specs=[VMEM_SPEC] * 5,
            out_specs=VMEM_SPEC,
            compiler_params=params(),
        )(maxima, sums, acts, gain, bias)
        blocks = lax.all_to_all(page, "mp", 0, 0, tiled=True)
    with jax.named_scope("smoothed_weight"):
        served, scale, tok = pl.pallas_call(
            serve_kernel,
            out_shape=(
                jax.ShapeDtypeStruct((48, D), jnp.bfloat16),
                jax.ShapeDtypeStruct((12, 128), jnp.float32),
                jax.ShapeDtypeStruct((4, 128), jnp.float32),
            ),
            in_specs=[SMEM_SPEC, VMEM_SPEC, VMEM_SPEC],
            out_specs=(ANY_SPEC, VMEM_SPEC, VMEM_SPEC),
            scratch_shapes=[pltpu.VMEM((48, D), jnp.bfloat16), pltpu.SemaphoreType.DMA((4,))],
            compiler_params=params(),
        )(lengths, blocks, pages)
    return served, scale.reshape(1536), tok.reshape(512)


def solution(mesh):
    return jax.shard_map(
        body,
        mesh=mesh,
        in_specs=(P("dp", "mp"), P("dp"), P("mp"), P("mp"), P("dp", "mp")),
        out_specs=(P(("mp", "dp"), None), P("mp"), P("dp")),
        check_vma=False,
    )
```

```python
import jax
import jax.numpy as jnp
from jax import lax
from jax.experimental import pallas as pl
from jax.experimental.pallas import tpu as pltpu
from jax.sharding import PartitionSpec as P

D = 12288
SLOT = 256
EPS = 1e-05
VMEM_SPEC = pl.BlockSpec(memory_space=pltpu.VMEM)
SMEM_SPEC = pl.BlockSpec(memory_space=pltpu.SMEM)
ANY_SPEC = pl.BlockSpec(memory_space=pl.ANY)


def params(mebibytes=40):
    return pltpu.CompilerParams(vmem_limit_bytes=mebibytes * 1024 * 1024)


def pack_kernel(w_hbm, page_hbm, peak_ref, w_ref, page_ref, rows_ref, in_sems, out_sems):
    parity = lax.axis_index("dp") % 2
    low = lax.broadcasted_iota(jnp.int32, (24, 128), 1) < 64
    first = low == (parity == 0)
    own = pl.ds(pl.multiple_of(192 * parity, 64), 192)

    def columns(step):
        return pl.ds(pl.multiple_of(384 * step, 128), 384)

    def fetch(step):
        return pltpu.make_async_copy(w_hbm.at[:, columns(step)], w_ref.at[:, columns(step)], in_sems.at[step])

    def store(step):
        peers = pl.ds(8 * step, 8)
        return pltpu.make_async_copy(page_ref.at[peers], page_hbm.at[peers], out_sems.at[step])

    for step in range(8):
        fetch(step).start()
    rows_ref[...] = jnp.zeros_like(rows_ref)

    def pack(step, carry):
        fetch(step).wait()
        w = jnp.abs(w_ref[:, columns(step)].astype(jnp.float32))
        peak = jnp.maximum(jnp.maximum(w[:, 0:128], w[:, 128:256]), w[:, 256:384])
        rows_ref[own, :] = jnp.maximum(rows_ref[own, :], peak)
        full = w_ref[pl.ds(pl.multiple_of(64 * parity, 64), 128), columns(step)].astype(jnp.float32).T
        half = w_ref[pl.ds(pl.multiple_of(128 * (1 - parity), 64), 64), columns(step)].astype(jnp.float32)
        twice = jnp.concatenate([half, half], axis=0).T
        for peer in range(8):
            upper = twice[48 * peer : 48 * peer + 24]
            lower = twice[48 * peer + 24 : 48 * peer + 48]
            page = jnp.concatenate([full[48 * peer : 48 * peer + 48], jnp.where(first, upper, lower)], axis=0)
            page_ref[8 * step + peer] = page.astype(jnp.bfloat16)
        store(step).start()
        return carry

    lax.fori_loop(0, 8, pack, 0)
    for block in range(3):
        peak_ref[block : block + 1, :] = jnp.max(rows_ref[pl.ds(128 * block, 128), :].T, axis=0, keepdims=True)
    peak_ref[3:8, :] = jnp.zeros((5, 128), jnp.float32)
    for step in range(8):
        store(step).wait()


def stats_kernel(peak_ref, acts_ref, page_ref):
    page_ref[8:16, :] = peak_ref[...]
    for block in range(4):
        total = jnp.zeros((128, 128), jnp.float32)
        square = jnp.zeros((128, 128), jnp.float32)
        for tile in range(12):
            x = acts_ref[pl.ds(128 * block, 128), pl.ds(128 * tile, 128)].astype(jnp.float32)
            total = total + x
            square = square + x * x
        page_ref[block : block + 1, :] = jnp.sum(total.T, axis=0, keepdims=True)
        page_ref[4 + block : 5 + block, :] = jnp.sum(square.T, axis=0, keepdims=True)


def moments(sums):
    mean = sums[0:4] / D
    var = sums[4:8] / D - mean * mean
    rstd = lax.rsqrt(var + EPS)
    return jnp.concatenate([mean, rstd], axis=0).T


def act_kernel(lengths_ref, sums_ref, acts_ref, gain_ref, bias_ref, page_ref):
    columns = moments(sums_ref[...])
    place = lax.broadcasted_iota(jnp.int32, (128, 128), 0)
    peaks = [jnp.zeros((8, 128), jnp.float32)] * 12
    for block in range(4):
        mean = jnp.broadcast_to(columns[:, block : block + 1], (128, 128))
        rstd = jnp.broadcast_to(columns[:, 4 + block : 5 + block], (128, 128))
        valid = place + 128 * (block % 2) < lengths_ref[block // 2]
        for tile in range(12):
            x = acts_ref[pl.ds(128 * block, 128), pl.ds(128 * tile, 128)].astype(jnp.float32)
            normed = (x - mean) * rstd * gain_ref[tile : tile + 1, :] + bias_ref[tile : tile + 1, :]
            peak = jnp.where(valid, jnp.abs(normed), 0.0)
            peaks[tile] = jnp.maximum(peaks[tile], jnp.max(peak.reshape(16, 8, 128), axis=0))
    for tile in range(12):
        page_ref[tile : tile + 1, :] = jnp.max(peaks[tile], axis=0, keepdims=True)
    page_ref[12:15, :] = sums_ref[8:11, :]
    page_ref[15:16, :] = jnp.zeros((1, 128), jnp.float32)


def peak_kernel(maxima_ref, sums_ref, acts_ref, gain_ref, bias_ref, page_ref):
    columns = moments(sums_ref[...])
    start = 4 * lax.axis_index("mp")
    act = jnp.max(maxima_ref[:, 0:12, :], axis=0)
    for slot in range(4):
        page_ref[0, 3 * slot : 3 * slot + 3, :] = maxima_ref[start + slot, 12:15, :]
    scale = jnp.sqrt(act + EPS) / jnp.sqrt(page_ref[0, 0:12, :] + EPS)
    page_ref[0, 0:12, :] = scale
    inverse = 1.0 / scale
    gain = gain_ref[...] * inverse
    bias = bias_ref[...] * inverse
    for block in range(4):
        mean = jnp.broadcast_to(columns[:, block : block + 1], (128, 128))
        rstd = jnp.broadcast_to(columns[:, 4 + block : 5 + block], (128, 128))
        peak = jnp.zeros((128, 128), jnp.float32)
        for tile in range(12):
            x = acts_ref[pl.ds(128 * block, 128), pl.ds(128 * tile, 128)].astype(jnp.float32)
            smoothed = (x - mean) * rstd * gain[tile : tile + 1] + bias[tile : tile + 1]
            peak = jnp.maximum(peak, jnp.abs(smoothed))
        page_ref[0, 12 + block : 13 + block, :] = jnp.max(peak.T, axis=0, keepdims=True)
    page = page_ref[0]
    for peer in range(1, page_ref.shape[0]):
        page_ref[peer] = page


def unpack_kernel(own_ref, other_ref, raw_ref):
    core = lax.axis_index("dp") % 2
    low = lax.broadcasted_iota(jnp.int32, (24, 128), 1) < 64
    first = low == (core == 0)

    def unpack(chip, carry):
        own = own_ref[2 * chip + core].astype(jnp.float32)
        other = other_ref[chip].astype(jnp.float32)
        upper = jnp.where(first, own[48:72], other[48:72])
        lower = pltpu.roll(jnp.where(first, other[48:72], own[48:72]), 64, 1)
        even = jnp.where(core == 0, own[0:48], other[0:48])
        odd = jnp.where(core == 0, other[0:48], own[0:48])
        triple = jnp.concatenate([even, jnp.concatenate([upper, lower], axis=0), odd], axis=1)
        raw_ref[:, pl.ds(pl.multiple_of(384 * chip, 128), 384)] = triple.astype(jnp.bfloat16)
        return carry

    lax.fori_loop(0, 32, unpack, 0, unroll=4)


def serve_kernel(lengths_ref, blocks_ref, raw_ref, served_hbm, scale_ref, tok_ref, served_ref, sems):
    def store(step):
        columns = pl.ds(3072 * step, 3072)
        return pltpu.make_async_copy(served_ref.at[:, columns], served_hbm.at[:, columns], sems.at[step])

    for step in range(4):
        for row in range(24 * step, 24 * step + 24):
            scale = blocks_ref[row // 12, row % 12 : row % 12 + 1, :]
            columns = pl.ds(128 * row, 128)
            served_ref[:, columns] = (raw_ref[:, columns].astype(jnp.float32) * scale).astype(jnp.bfloat16)
        store(step).start()
    scale_ref[...] = blocks_ref[lax.axis_index("mp"), 0:12, :]
    peaks = jnp.max(blocks_ref[:, 12:16, :], axis=0)
    lane = lax.broadcasted_iota(jnp.int32, (1, 128), 1)
    for block in range(4):
        valid = lane + 128 * (block % 2) < lengths_ref[block // 2]
        tok_ref[block : block + 1, :] = jnp.where(valid, peaks[block : block + 1], 0.0)
    for step in range(4):
        store(step).wait()


def swap(x, axis, bit):
    size = lax.axis_size(axis)
    return lax.ppermute(x, axis, [(i, i ^ bit) for i in range(size)])


def body(acts, lengths, ln_gain, ln_bias, w_fc1):
    gain = ln_gain.reshape(12, 128)
    bias = ln_bias.reshape(12, 128)
    with jax.named_scope("weight_exchange"):
        packed, w_peak = pl.pallas_call(
            pack_kernel,
            out_shape=(
                jax.ShapeDtypeStruct((64, 72, 128), jnp.bfloat16),
                jax.ShapeDtypeStruct((8, 128), jnp.float32),
            ),
            in_specs=[ANY_SPEC],
            out_specs=(ANY_SPEC, VMEM_SPEC),
            scratch_shapes=[
                pltpu.VMEM((192, 3072), jnp.bfloat16),
                pltpu.VMEM((64, 72, 128), jnp.bfloat16),
                pltpu.VMEM((384, 128), jnp.float32),
                pltpu.SemaphoreType.DMA((8,)),
                pltpu.SemaphoreType.DMA((8,)),
            ],
            compiler_params=params(60),
        )(w_fc1)
        kinds = [[2 * chip + core for chip in range(32)] for core in range(2)]
        pages = lax.all_to_all(packed, "dp", 0, 0, axis_index_groups=kinds, tiled=True)
    with jax.named_scope("token_moments"):
        sums = pl.pallas_call(
            stats_kernel,
            out_shape=jax.ShapeDtypeStruct((16, 128), jnp.float32),
            in_specs=[VMEM_SPEC, VMEM_SPEC],
            out_specs=VMEM_SPEC,
            compiler_params=params(),
        )(w_peak, acts)
        added = lax.broadcasted_iota(jnp.int32, (16, 128), 0) < 8
        for bit in (1, 2, 4):
            other = swap(sums, "mp", bit)
            sums = jnp.where(added, sums + other, jnp.maximum(sums, other))
    with jax.named_scope("channel_maxima"):
        maxima = pl.pallas_call(
            act_kernel,
            out_shape=jax.ShapeDtypeStruct((16, 128), jnp.float32),
            in_specs=[SMEM_SPEC] + [VMEM_SPEC] * 4,
            out_specs=VMEM_SPEC,
            compiler_params=params(),
        )(lengths, sums, acts, gain, bias)
        maxima = jnp.maximum(maxima, swap(maxima, "dp", 1))
        maxima, pages = lax.optimization_barrier((maxima, pages))
        copies = jnp.broadcast_to(maxima[None], (32, 16, 128))
        maxima = lax.all_to_all(copies, "dp", 0, 0, axis_index_groups=kinds, tiled=True)
    with jax.named_scope("core_halves"):
        core = lax.axis_index("dp") % 2
        theirs = lax.dynamic_index_in_dim(pages.reshape(32, 2, 72, 128), 1 - core, 1, keepdims=False)
        others = swap(theirs, "dp", 1)
        raw = pl.pallas_call(
            unpack_kernel,
            out_shape=jax.ShapeDtypeStruct((48, D), jnp.bfloat16),
            in_specs=[VMEM_SPEC, VMEM_SPEC],
            out_specs=VMEM_SPEC,
            compiler_params=params(),
        )(pages, others)
    with jax.named_scope("token_peaks"):
        page = pl.pallas_call(
            peak_kernel,
            out_shape=jax.ShapeDtypeStruct((8, 16, 128), jnp.float32),
            in_specs=[VMEM_SPEC] * 5,
            out_specs=VMEM_SPEC,
            compiler_params=params(),
        )(maxima, sums, acts, gain, bias)
        blocks = lax.all_to_all(page, "mp", 0, 0, tiled=True)
    with jax.named_scope("smoothed_weight"):
        served, scale, tok = pl.pallas_call(
            serve_kernel,
            out_shape=(
                jax.ShapeDtypeStruct((48, D), jnp.bfloat16),
                jax.ShapeDtypeStruct((12, 128), jnp.float32),
                jax.ShapeDtypeStruct((4, 128), jnp.float32),
            ),
            in_specs=[SMEM_SPEC, VMEM_SPEC, VMEM_SPEC],
            out_specs=(ANY_SPEC, VMEM_SPEC, VMEM_SPEC),
            scratch_shapes=[pltpu.VMEM((48, D), jnp.bfloat16), pltpu.SemaphoreType.DMA((4,))],
            compiler_params=params(),
        )(lengths, blocks, raw)
    return served, scale.reshape(1536), tok.reshape(512)


def solution(mesh):
    return jax.shard_map(
        body,
        mesh=mesh,
        in_specs=(P("dp", "mp"), P("dp"), P("mp"), P("mp"), P("dp", "mp")),
        out_specs=(P(("mp", "dp"), None), P("mp"), P("dp")),
        check_vma=False,
    )
```

```python
import jax
import jax.numpy as jnp
from jax import lax
from jax.experimental import pallas as pl
from jax.experimental.pallas import tpu as pltpu
from jax.sharding import PartitionSpec as P

D = 12288
SLOT = 256
EPS = 1e-05
VMEM_SPEC = pl.BlockSpec(memory_space=pltpu.VMEM)
SMEM_SPEC = pl.BlockSpec(memory_space=pltpu.SMEM)
ANY_SPEC = pl.BlockSpec(memory_space=pl.ANY)


def params(mebibytes=40):
    return pltpu.CompilerParams(vmem_limit_bytes=mebibytes * 1024 * 1024)


def stats_kernel(acts_hbm, w_hbm, page_ref, acts_ref, w_ref, rows_ref, acts_sems, w_sems):
    parity = lax.axis_index("dp") % 2
    acts_copies, w_copies = [], []
    for block in range(4):
        tokens, rows = pl.ds(128 * block, 128), pl.ds(48 * block, 48)
        acts_copies.append(pltpu.make_async_copy(acts_hbm.at[tokens], acts_ref.at[tokens], acts_sems.at[block]))
        w_copies.append(pltpu.make_async_copy(w_hbm.at[rows], w_ref.at[rows], w_sems.at[block]))
    for copy in w_copies + acts_copies:
        copy.start()
    rows_ref[...] = jnp.zeros_like(rows_ref)
    for block in range(4):
        w_copies[block].wait()
        peak = jnp.zeros((48, 128), jnp.float32)
        for tile in range(24):
            peak = jnp.maximum(peak, jnp.abs(w_ref[pl.ds(48 * block, 48), pl.ds(128 * tile, 128)].astype(jnp.float32)))
        rows_ref[pl.ds(pl.multiple_of(192 * parity + 48 * block, 16), 48), :] = peak
    for block in range(3):
        page_ref[0, 8 + block : 9 + block, :] = jnp.max(rows_ref[pl.ds(128 * block, 128), :].T, axis=0, keepdims=True)
    page_ref[0, 11:16, :] = jnp.zeros((5, 128), jnp.float32)
    for block in range(4):
        acts_copies[block].wait()
        total = jnp.zeros((128, 128), jnp.float32)
        square = jnp.zeros((128, 128), jnp.float32)
        for tile in range(12):
            x = acts_ref[pl.ds(128 * block, 128), pl.ds(128 * tile, 128)].astype(jnp.float32)
            total = total + x
            square = square + x * x
        page_ref[0, block : block + 1, :] = jnp.sum(total.T, axis=0, keepdims=True)
        page_ref[0, 4 + block : 5 + block, :] = jnp.sum(square.T, axis=0, keepdims=True)
    page = page_ref[0]
    for peer in range(1, page_ref.shape[0]):
        page_ref[peer] = page


def pack_kernel(w_hbm, page_hbm, w_ref, page_ref, in_sems, out_sems):
    parity = lax.axis_index("dp") % 2
    low = lax.broadcasted_iota(jnp.int32, (24, 128), 1) < 64
    first = low == (parity == 0)

    def columns(step):
        return pl.ds(pl.multiple_of(384 * step, 128), 384)

    def fetch(step):
        return pltpu.make_async_copy(w_hbm.at[:, columns(step)], w_ref.at[:, columns(step)], in_sems.at[step])

    def store(step):
        peers = pl.ds(8 * step, 8)
        return pltpu.make_async_copy(page_ref.at[peers], page_hbm.at[peers], out_sems.at[step])

    for step in range(8):
        fetch(step).start()

    def pack(step, carry):
        fetch(step).wait()
        full = w_ref[pl.ds(pl.multiple_of(64 * parity, 64), 128), columns(step)].astype(jnp.float32).T
        half = w_ref[pl.ds(pl.multiple_of(128 * (1 - parity), 64), 64), columns(step)].astype(jnp.float32)
        twice = jnp.concatenate([half, half], axis=0).T
        for peer in range(8):
            upper = twice[48 * peer : 48 * peer + 24]
            lower = twice[48 * peer + 24 : 48 * peer + 48]
            page = jnp.concatenate([full[48 * peer : 48 * peer + 48], jnp.where(first, upper, lower)], axis=0)
            page_ref[8 * step + peer] = page.astype(jnp.bfloat16)
        store(step).start()
        return carry

    lax.fori_loop(0, 8, pack, 0)
    for step in range(8):
        store(step).wait()


def moments(sums):
    mean = sums[0:4] / D
    var = sums[4:8] / D - mean * mean
    rstd = lax.rsqrt(var + EPS)
    return jnp.concatenate([mean, rstd], axis=0).T


def act_kernel(lengths_ref, sums_ref, acts_ref, gain_ref, bias_ref, page_ref):
    columns = moments(sums_ref[...])
    place = lax.broadcasted_iota(jnp.int32, (128, 128), 0)
    peaks = [jnp.zeros((8, 128), jnp.float32)] * 12
    for block in range(4):
        mean = jnp.broadcast_to(columns[:, block : block + 1], (128, 128))
        rstd = jnp.broadcast_to(columns[:, 4 + block : 5 + block], (128, 128))
        valid = place + 128 * (block % 2) < lengths_ref[block // 2]
        for tile in range(12):
            x = acts_ref[pl.ds(128 * block, 128), pl.ds(128 * tile, 128)].astype(jnp.float32)
            normed = (x - mean) * rstd * gain_ref[tile : tile + 1, :] + bias_ref[tile : tile + 1, :]
            peak = jnp.where(valid, jnp.abs(normed), 0.0)
            peaks[tile] = jnp.maximum(peaks[tile], jnp.max(peak.reshape(16, 8, 128), axis=0))
    for tile in range(12):
        page_ref[tile : tile + 1, :] = jnp.max(peaks[tile], axis=0, keepdims=True)
    place = lax.axis_index("dp")
    for slot in range(4):
        kept = (place // 8 == lax.axis_index("mp")) & (place // 2 % 4 == slot)
        page_ref[12 + 3 * slot : 15 + 3 * slot, :] = jnp.where(kept, sums_ref[8:11, :], 0.0)


def peak_kernel(maxima_ref, sums_ref, acts_ref, gain_ref, bias_ref, page_ref):
    columns = moments(sums_ref[...])
    maxima = jnp.max(maxima_ref[...], axis=0)
    scale = jnp.sqrt(maxima[0:12] + EPS) / jnp.sqrt(maxima[12:24] + EPS)
    page_ref[0, 0:12, :] = scale
    inverse = 1.0 / scale
    gain = gain_ref[...] * inverse
    bias = bias_ref[...] * inverse
    for block in range(4):
        mean = jnp.broadcast_to(columns[:, block : block + 1], (128, 128))
        rstd = jnp.broadcast_to(columns[:, 4 + block : 5 + block], (128, 128))
        peak = jnp.zeros((128, 128), jnp.float32)
        for tile in range(12):
            x = acts_ref[pl.ds(128 * block, 128), pl.ds(128 * tile, 128)].astype(jnp.float32)
            smoothed = (x - mean) * rstd * gain[tile : tile + 1] + bias[tile : tile + 1]
            peak = jnp.maximum(peak, jnp.abs(smoothed))
        page_ref[0, 12 + block : 13 + block, :] = jnp.max(peak.T, axis=0, keepdims=True)
    page = page_ref[0]
    for peer in range(1, page_ref.shape[0]):
        page_ref[peer] = page


def serve_kernel(lengths_ref, blocks_ref, pages_ref, served_hbm, scale_ref, tok_ref, served_ref, sems):
    low = lax.broadcasted_iota(jnp.int32, (24, 128), 1) < 64

    def store(step):
        columns = pl.ds(pl.multiple_of(3072 * step, 128), 3072)
        return pltpu.make_async_copy(served_ref.at[:, columns], served_hbm.at[:, columns], sems.at[step])

    for step in range(4):
        for pair in range(8 * step, 8 * step + 8):
            even = pages_ref[2 * pair].astype(jnp.float32)
            odd = pages_ref[2 * pair + 1].astype(jnp.float32)
            upper = jnp.where(low, even[48:72], odd[48:72])
            lower = pltpu.roll(jnp.where(low, odd[48:72], even[48:72]), 64, 1)
            middle = jnp.concatenate([upper, lower], axis=0)
            for part, tile in enumerate((even[0:48], middle, odd[0:48])):
                row = 3 * pair + part
                scale = blocks_ref[row // 12, row % 12 : row % 12 + 1, :]
                served_ref[:, pl.ds(128 * row, 128)] = (tile * scale).astype(jnp.bfloat16)
        store(step).start()
    scale_ref[...] = blocks_ref[lax.axis_index("mp"), 0:12, :]
    peaks = jnp.max(blocks_ref[:, 12:16, :], axis=0)
    lane = lax.broadcasted_iota(jnp.int32, (1, 128), 1)
    for block in range(4):
        valid = lane + 128 * (block % 2) < lengths_ref[block // 2]
        tok_ref[block : block + 1, :] = jnp.where(valid, peaks[block : block + 1], 0.0)
    for step in range(4):
        store(step).wait()


def swap(x, axis, bit):
    size = lax.axis_size(axis)
    return lax.ppermute(x, axis, [(i, i ^ bit) for i in range(size)])


def body(acts, lengths, ln_gain, ln_bias, w_fc1):
    gain = ln_gain.reshape(12, 128)
    bias = ln_bias.reshape(12, 128)
    with jax.named_scope("token_moments"):
        page = pl.pallas_call(
            stats_kernel,
            out_shape=jax.ShapeDtypeStruct((4, 16, 128), jnp.float32),
            in_specs=[ANY_SPEC, ANY_SPEC],
            out_specs=VMEM_SPEC,
            scratch_shapes=[
                pltpu.VMEM((512, 1536), jnp.bfloat16),
                pltpu.VMEM((192, 3072), jnp.bfloat16),
                pltpu.VMEM((384, 128), jnp.float32),
                pltpu.SemaphoreType.DMA((4,)),
                pltpu.SemaphoreType.DMA((4,)),
            ],
            compiler_params=params(60),
        )(acts, w_fc1)
        parts = lax.all_to_all(page, "mp", 0, 0, axis_index_groups=[[0, 1, 2, 3], [4, 5, 6, 7]], tiled=True)
    with jax.named_scope("weight_exchange"):
        packed = pl.pallas_call(
            pack_kernel,
            out_shape=jax.ShapeDtypeStruct((64, 72, 128), jnp.bfloat16),
            in_specs=[ANY_SPEC],
            out_specs=ANY_SPEC,
            scratch_shapes=[
                pltpu.VMEM((192, 3072), jnp.bfloat16),
                pltpu.VMEM((64, 72, 128), jnp.bfloat16),
                pltpu.SemaphoreType.DMA((8,)),
                pltpu.SemaphoreType.DMA((8,)),
            ],
            compiler_params=params(60),
        )(w_fc1)
        packed, parts = lax.optimization_barrier((packed, parts))
        pages = lax.all_to_all(packed, "dp", 0, 0, tiled=True)
    with jax.named_scope("channel_maxima"):
        added = lax.broadcasted_iota(jnp.int32, (16, 128), 0) < 8
        sums = jnp.where(added, jnp.sum(parts, axis=0), jnp.max(parts, axis=0))
        other = swap(sums, "mp", 4)
        sums = jnp.where(added, sums + other, jnp.maximum(sums, other))
        maxima = pl.pallas_call(
            act_kernel,
            out_shape=jax.ShapeDtypeStruct((24, 128), jnp.float32),
            in_specs=[SMEM_SPEC] + [VMEM_SPEC] * 4,
            out_specs=VMEM_SPEC,
            compiler_params=params(),
        )(lengths, sums, acts, gain, bias)
        for bit in (1, 2, 4, 8):
            maxima = jnp.maximum(maxima, swap(maxima, "dp", bit))
        maxima, pages = lax.optimization_barrier((maxima, pages))
        copies = jnp.broadcast_to(maxima[None], (4, 24, 128))
        kinds = [[16 * pair + rest for pair in range(4)] for rest in range(16)]
        maxima = lax.all_to_all(copies, "dp", 0, 0, axis_index_groups=kinds, tiled=True)
    with jax.named_scope("token_peaks"):
        page = pl.pallas_call(
            peak_kernel,
            out_shape=jax.ShapeDtypeStruct((8, 16, 128), jnp.float32),
            in_specs=[VMEM_SPEC] * 5,
            out_specs=VMEM_SPEC,
            compiler_params=params(),
        )(maxima, sums, acts, gain, bias)
        blocks = lax.all_to_all(page, "mp", 0, 0, tiled=True)
    with jax.named_scope("smoothed_weight"):
        served, scale, tok = pl.pallas_call(
            serve_kernel,
            out_shape=(
                jax.ShapeDtypeStruct((48, D), jnp.bfloat16),
                jax.ShapeDtypeStruct((12, 128), jnp.float32),
                jax.ShapeDtypeStruct((4, 128), jnp.float32),
            ),
            in_specs=[SMEM_SPEC, VMEM_SPEC, VMEM_SPEC],
            out_specs=(ANY_SPEC, VMEM_SPEC, VMEM_SPEC),
            scratch_shapes=[pltpu.VMEM((48, D), jnp.bfloat16), pltpu.SemaphoreType.DMA((4,))],
            compiler_params=params(),
        )(lengths, blocks, pages)
    return served, scale.reshape(1536), tok.reshape(512)


def solution(mesh):
    return jax.shard_map(
        body,
        mesh=mesh,
        in_specs=(P("dp", "mp"), P("dp"), P("mp"), P("mp"), P("dp", "mp")),
        out_specs=(P(("mp", "dp"), None), P("mp"), P("dp")),
        check_vma=False,
    )
```

```python
import jax
import jax.numpy as jnp
from jax import lax
from jax.experimental import pallas as pl
from jax.experimental.pallas import tpu as pltpu
from jax.sharding import PartitionSpec as P

D = 12288
SLOT = 256
EPS = 1e-05
VMEM_SPEC = pl.BlockSpec(memory_space=pltpu.VMEM)
SMEM_SPEC = pl.BlockSpec(memory_space=pltpu.SMEM)
ANY_SPEC = pl.BlockSpec(memory_space=pl.ANY)


def params(mebibytes=40):
    return pltpu.CompilerParams(vmem_limit_bytes=mebibytes * 1024 * 1024)


def pack_kernel(w_hbm, page_hbm, peak_ref, w_ref, page_ref, rows_ref, in_sems, out_sems):
    parity = lax.axis_index("dp") % 2
    low = lax.broadcasted_iota(jnp.int32, (24, 128), 1) < 64
    first = low == (parity == 0)

    def columns(step):
        return pl.ds(pl.multiple_of(384 * step, 128), 384)

    def fetch(step):
        return pltpu.make_async_copy(w_hbm.at[:, columns(step)], w_ref.at[:, columns(step)], in_sems.at[step])

    def store(step):
        peers = pl.ds(8 * step, 8)
        return pltpu.make_async_copy(page_ref.at[peers], page_hbm.at[peers], out_sems.at[step])

    for step in range(8):
        fetch(step).start()
    rows_ref[...] = jnp.zeros_like(rows_ref)
    own = pl.ds(pl.multiple_of(192 * parity, 64), 192)

    def pack(step, carry):
        fetch(step).wait()
        w = jnp.abs(w_ref[:, columns(step)])
        peak = jnp.maximum(jnp.maximum(w[:, 0:128], w[:, 128:256]), w[:, 256:384])
        rows_ref[own, :] = jnp.maximum(rows_ref[own, :], peak)
        full = w_ref[pl.ds(pl.multiple_of(64 * parity, 64), 128), columns(step)].T
        half = w_ref[pl.ds(pl.multiple_of(128 * (1 - parity), 64), 64), columns(step)]
        twice = jnp.concatenate([half, half], axis=0).T.astype(jnp.float32)
        for peer in range(8):
            upper = twice[48 * peer : 48 * peer + 24]
            lower = twice[48 * peer + 24 : 48 * peer + 48]
            halves = jnp.where(first, upper, lower).astype(jnp.bfloat16)
            page_ref[8 * step + peer] = jnp.concatenate([full[48 * peer : 48 * peer + 48], halves], axis=0)
        store(step).start()
        return carry

    lax.fori_loop(0, 8, pack, 0)
    for block in range(3):
        rows = rows_ref[pl.ds(128 * block, 128), :].astype(jnp.float32)
        peak_ref[block : block + 1, :] = jnp.max(rows.T, axis=0, keepdims=True)
    peak_ref[3:8, :] = jnp.zeros((5, 128), jnp.float32)
    for step in range(8):
        store(step).wait()


def stats_kernel(peak_ref, acts_ref, page_ref):
    page_ref[8:16, :] = peak_ref[...]
    for block in range(4):
        total = jnp.zeros((128, 128), jnp.float32)
        square = jnp.zeros((128, 128), jnp.float32)
        for tile in range(12):
            x = acts_ref[pl.ds(128 * block, 128), pl.ds(128 * tile, 128)].astype(jnp.float32)
            total = total + x
            square = square + x * x
        page_ref[block : block + 1, :] = jnp.sum(total.T, axis=0, keepdims=True)
        page_ref[4 + block : 5 + block, :] = jnp.sum(square.T, axis=0, keepdims=True)


def moments(sums):
    mean = sums[0:4] / D
    var = sums[4:8] / D - mean * mean
    rstd = lax.rsqrt(var + EPS)
    return jnp.concatenate([mean, rstd], axis=0).T


def act_kernel(lengths_ref, sums_ref, acts_ref, gain_ref, bias_ref, page_ref):
    columns = moments(sums_ref[...])
    place = lax.broadcasted_iota(jnp.int32, (128, 128), 0)
    peaks = [jnp.zeros((8, 128), jnp.float32)] * 12
    for block in range(4):
        mean = jnp.broadcast_to(columns[:, block : block + 1], (128, 128))
        rstd = jnp.broadcast_to(columns[:, 4 + block : 5 + block], (128, 128))
        valid = place + 128 * (block % 2) < lengths_ref[block // 2]
        for tile in range(12):
            x = acts_ref[pl.ds(128 * block, 128), pl.ds(128 * tile, 128)].astype(jnp.float32)
            normed = (x - mean) * rstd * gain_ref[tile : tile + 1, :] + bias_ref[tile : tile + 1, :]
            peak = jnp.where(valid, jnp.abs(normed), 0.0)
            peaks[tile] = jnp.maximum(peaks[tile], jnp.max(peak.reshape(16, 8, 128), axis=0))
    for tile in range(12):
        page_ref[tile : tile + 1, :] = jnp.max(peaks[tile], axis=0, keepdims=True)
    page_ref[12:15, :] = sums_ref[8:11, :]
    page_ref[15:16, :] = jnp.zeros((1, 128), jnp.float32)


def peak_kernel(maxima_ref, sums_ref, acts_ref, gain_ref, bias_ref, page_ref):
    columns = moments(sums_ref[...])
    start = 4 * lax.axis_index("mp")
    act = jnp.max(maxima_ref[:, 0:12, :], axis=0)
    for slot in range(4):
        page_ref[0, 3 * slot : 3 * slot + 3, :] = maxima_ref[start + slot, 12:15, :]
    scale = jnp.sqrt(act + EPS) / jnp.sqrt(page_ref[0, 0:12, :] + EPS)
    page_ref[0, 0:12, :] = scale
    inverse = 1.0 / scale
    gain = gain_ref[...] * inverse
    bias = bias_ref[...] * inverse
    for block in range(4):
        mean = jnp.broadcast_to(columns[:, block : block + 1], (128, 128))
        rstd = jnp.broadcast_to(columns[:, 4 + block : 5 + block], (128, 128))
        peak = jnp.zeros((128, 128), jnp.float32)
        for tile in range(12):
            x = acts_ref[pl.ds(128 * block, 128), pl.ds(128 * tile, 128)].astype(jnp.float32)
            smoothed = (x - mean) * rstd * gain[tile : tile + 1] + bias[tile : tile + 1]
            peak = jnp.maximum(peak, jnp.abs(smoothed))
        page_ref[0, 12 + block : 13 + block, :] = jnp.max(peak.T, axis=0, keepdims=True)
    page = page_ref[0]
    for peer in range(1, page_ref.shape[0]):
        page_ref[peer] = page


def serve_kernel(lengths_ref, blocks_ref, pages_ref, served_hbm, scale_ref, tok_ref, served_ref, sems):
    low = lax.broadcasted_iota(jnp.int32, (24, 128), 1) < 64

    def store(step):
        columns = pl.ds(1536 * step, 1536)
        return pltpu.make_async_copy(served_ref.at[:, columns], served_hbm.at[:, columns], sems.at[step])

    for step in range(8):
        for pair in range(4 * step, 4 * step + 4):
            even = pages_ref[2 * pair].astype(jnp.float32)
            odd = pages_ref[2 * pair + 1].astype(jnp.float32)
            upper = jnp.where(low, even[48:72], odd[48:72])
            lower = pltpu.roll(jnp.where(low, odd[48:72], even[48:72]), 64, 1)
            middle = jnp.concatenate([upper, lower], axis=0)
            for part, tile in enumerate((even[0:48], middle, odd[0:48])):
                row = 3 * pair + part
                scale = blocks_ref[row // 12, row % 12 : row % 12 + 1, :]
                served_ref[:, pl.ds(128 * row, 128)] = (tile * scale).astype(jnp.bfloat16)
        store(step).start()
    scale_ref[...] = blocks_ref[lax.axis_index("mp"), 0:12, :]
    peaks = jnp.max(blocks_ref[:, 12:16, :], axis=0)
    lane = lax.broadcasted_iota(jnp.int32, (1, 128), 1)
    for block in range(4):
        valid = lane + 128 * (block % 2) < lengths_ref[block // 2]
        tok_ref[block : block + 1, :] = jnp.where(valid, peaks[block : block + 1], 0.0)
    for step in range(8):
        store(step).wait()


def swap(x, axis, bit):
    size = lax.axis_size(axis)
    return lax.ppermute(x, axis, [(i, i ^ bit) for i in range(size)])


def body(acts, lengths, ln_gain, ln_bias, w_fc1):
    gain = ln_gain.reshape(12, 128)
    bias = ln_bias.reshape(12, 128)
    with jax.named_scope("weight_exchange"):
        packed, w_peak = pl.pallas_call(
            pack_kernel,
            out_shape=(
                jax.ShapeDtypeStruct((64, 72, 128), jnp.bfloat16),
                jax.ShapeDtypeStruct((8, 128), jnp.float32),
            ),
            in_specs=[ANY_SPEC],
            out_specs=(ANY_SPEC, VMEM_SPEC),
            scratch_shapes=[
                pltpu.VMEM((192, 3072), jnp.bfloat16),
                pltpu.VMEM((64, 72, 128), jnp.bfloat16),
                pltpu.VMEM((384, 128), jnp.bfloat16),
                pltpu.SemaphoreType.DMA((8,)),
                pltpu.SemaphoreType.DMA((8,)),
            ],
            compiler_params=params(60),
        )(w_fc1)
        pages = lax.all_to_all(packed, "dp", 0, 0, tiled=True)
    with jax.named_scope("token_moments"):
        sums = pl.pallas_call(
            stats_kernel,
            out_shape=jax.ShapeDtypeStruct((16, 128), jnp.float32),
            in_specs=[VMEM_SPEC, VMEM_SPEC],
            out_specs=VMEM_SPEC,
            compiler_params=params(),
        )(w_peak, acts)
        added = lax.broadcasted_iota(jnp.int32, (16, 128), 0) < 8
        for bit in (1, 2, 4):
            other = swap(sums, "mp", bit)
            sums = jnp.where(added, sums + other, jnp.maximum(sums, other))
    with jax.named_scope("channel_maxima"):
        maxima = pl.pallas_call(
            act_kernel,
            out_shape=jax.ShapeDtypeStruct((16, 128), jnp.float32),
            in_specs=[SMEM_SPEC] + [VMEM_SPEC] * 4,
            out_specs=VMEM_SPEC,
            compiler_params=params(),
        )(lengths, sums, acts, gain, bias)
        maxima = jnp.maximum(maxima, swap(maxima, "dp", 1))
        maxima, pages = lax.optimization_barrier((maxima, pages))
        copies = jnp.broadcast_to(maxima[None], (32, 16, 128))
        kinds = [[2 * chip + core for chip in range(32)] for core in range(2)]
        maxima = lax.all_to_all(copies, "dp", 0, 0, axis_index_groups=kinds, tiled=True)
    with jax.named_scope("token_peaks"):
        page = pl.pallas_call(
            peak_kernel,
            out_shape=jax.ShapeDtypeStruct((8, 16, 128), jnp.float32),
            in_specs=[VMEM_SPEC] * 5,
            out_specs=VMEM_SPEC,
            compiler_params=params(),
        )(maxima, sums, acts, gain, bias)
        blocks = lax.all_to_all(page, "mp", 0, 0, tiled=True)
    with jax.named_scope("smoothed_weight"):
        served, scale, tok = pl.pallas_call(
            serve_kernel,
            out_shape=(
                jax.ShapeDtypeStruct((48, D), jnp.bfloat16),
                jax.ShapeDtypeStruct((12, 128), jnp.float32),
                jax.ShapeDtypeStruct((4, 128), jnp.float32),
            ),
            in_specs=[SMEM_SPEC, VMEM_SPEC, VMEM_SPEC],
            out_specs=(ANY_SPEC, VMEM_SPEC, VMEM_SPEC),
            scratch_shapes=[pltpu.VMEM((48, D), jnp.bfloat16), pltpu.SemaphoreType.DMA((8,))],
            compiler_params=params(),
        )(lengths, blocks, pages)
    return served, scale.reshape(1536), tok.reshape(512)


def solution(mesh):
    return jax.shard_map(
        body,
        mesh=mesh,
        in_specs=(P("dp", "mp"), P("dp"), P("mp"), P("mp"), P("dp", "mp")),
        out_specs=(P(("mp", "dp"), None), P("mp"), P("dp")),
        check_vma=False,
    )
```

```python
import jax
import jax.numpy as jnp
from jax import lax
from jax.experimental import pallas as pl
from jax.experimental.pallas import tpu as pltpu
from jax.sharding import PartitionSpec as P

D = 12288
SLOT = 256
EPS = 1e-05
VMEM_SPEC = pl.BlockSpec(memory_space=pltpu.VMEM)
SMEM_SPEC = pl.BlockSpec(memory_space=pltpu.SMEM)
ANY_SPEC = pl.BlockSpec(memory_space=pl.ANY)


def params(mebibytes=40):
    return pltpu.CompilerParams(vmem_limit_bytes=mebibytes * 1024 * 1024)


def pack_kernel(w_hbm, page_hbm, w_ref, page_ref, in_sems, out_sems):
    parity = lax.axis_index("dp") % 2
    low = lax.broadcasted_iota(jnp.int32, (24, 128), 1) < 64
    first = low == (parity == 0)

    def columns(step):
        return pl.ds(pl.multiple_of(384 * step, 128), 384)

    def fetch(step):
        return pltpu.make_async_copy(w_hbm.at[:, columns(step)], w_ref.at[:, columns(step)], in_sems.at[step])

    def store(step):
        peers = pl.ds(8 * step, 8)
        return pltpu.make_async_copy(page_ref.at[peers], page_hbm.at[peers], out_sems.at[step])

    for step in range(8):
        fetch(step).start()

    def pack(step, carry):
        fetch(step).wait()
        full = w_ref[pl.ds(pl.multiple_of(64 * parity, 64), 128), columns(step)].T
        half = w_ref[pl.ds(pl.multiple_of(128 * (1 - parity), 64), 64), columns(step)]
        twice = jnp.concatenate([half, half], axis=0).T.astype(jnp.float32)
        for peer in range(8):
            upper = twice[48 * peer : 48 * peer + 24]
            lower = twice[48 * peer + 24 : 48 * peer + 48]
            halves = jnp.where(first, upper, lower).astype(jnp.bfloat16)
            page_ref[8 * step + peer] = jnp.concatenate([full[48 * peer : 48 * peer + 48], halves], axis=0)
        store(step).start()
        return carry

    lax.fori_loop(0, 8, pack, 0)
    for step in range(8):
        store(step).wait()


def stats_kernel(acts_ref, w_ref, page_ref, rows_ref):
    rows_ref[...] = jnp.zeros_like(rows_ref)
    peak = jnp.zeros((192, 128), jnp.bfloat16)
    for tile in range(24):
        peak = jnp.maximum(peak, jnp.abs(w_ref[:, pl.ds(128 * tile, 128)]))
    rows_ref[pl.ds(pl.multiple_of(192 * (lax.axis_index("dp") % 2), 64), 192), :] = peak.astype(jnp.float32)
    for block in range(3):
        page_ref[8 + block : 9 + block, :] = jnp.max(rows_ref[pl.ds(128 * block, 128), :].T, axis=0, keepdims=True)
    page_ref[11:16, :] = jnp.zeros((5, 128), jnp.float32)
    for block in range(4):
        total = jnp.zeros((128, 128), jnp.float32)
        square = jnp.zeros((128, 128), jnp.float32)
        for tile in range(12):
            x = acts_ref[pl.ds(128 * block, 128), pl.ds(128 * tile, 128)].astype(jnp.float32)
            total = total + x
            square = square + x * x
        page_ref[block : block + 1, :] = jnp.sum(total.T, axis=0, keepdims=True)
        page_ref[4 + block : 5 + block, :] = jnp.sum(square.T, axis=0, keepdims=True)


def moments(sums):
    mean = sums[0:4] / D
    var = sums[4:8] / D - mean * mean
    rstd = lax.rsqrt(var + EPS)
    return jnp.concatenate([mean, rstd], axis=0).T


def act_kernel(lengths_ref, sums_ref, acts_ref, gain_ref, bias_ref, page_ref):
    columns = moments(sums_ref[...])
    place = lax.broadcasted_iota(jnp.int32, (128, 128), 0)
    peaks = [jnp.zeros((8, 128), jnp.float32)] * 12
    for block in range(4):
        mean = jnp.broadcast_to(columns[:, block : block + 1], (128, 128))
        rstd = jnp.broadcast_to(columns[:, 4 + block : 5 + block], (128, 128))
        valid = place + 128 * (block % 2) < lengths_ref[block // 2]
        for tile in range(12):
            x = acts_ref[pl.ds(128 * block, 128), pl.ds(128 * tile, 128)].astype(jnp.float32)
            normed = (x - mean) * rstd * gain_ref[tile : tile + 1, :] + bias_ref[tile : tile + 1, :]
            peak = jnp.where(valid, jnp.abs(normed), 0.0)
            peaks[tile] = jnp.maximum(peaks[tile], jnp.max(peak.reshape(16, 8, 128), axis=0))
    for tile in range(12):
        page_ref[tile : tile + 1, :] = jnp.max(peaks[tile], axis=0, keepdims=True)
    page_ref[12:15, :] = sums_ref[8:11, :]
    page_ref[15:16, :] = jnp.zeros((1, 128), jnp.float32)


def peak_kernel(maxima_ref, sums_ref, acts_ref, gain_ref, bias_ref, page_ref):
    columns = moments(sums_ref[...])
    start = 4 * lax.axis_index("mp")
    act = jnp.max(maxima_ref[:, 0:12, :], axis=0)
    for slot in range(4):
        page_ref[0, 3 * slot : 3 * slot + 3, :] = maxima_ref[start + slot, 12:15, :]
    scale = jnp.sqrt(act + EPS) / jnp.sqrt(page_ref[0, 0:12, :] + EPS)
    page_ref[0, 0:12, :] = scale
    inverse = 1.0 / scale
    gain = gain_ref[...] * inverse
    bias = bias_ref[...] * inverse
    for block in range(4):
        mean = jnp.broadcast_to(columns[:, block : block + 1], (128, 128))
        rstd = jnp.broadcast_to(columns[:, 4 + block : 5 + block], (128, 128))
        peak = jnp.zeros((128, 128), jnp.float32)
        for tile in range(12):
            x = acts_ref[pl.ds(128 * block, 128), pl.ds(128 * tile, 128)].astype(jnp.float32)
            smoothed = (x - mean) * rstd * gain[tile : tile + 1] + bias[tile : tile + 1]
            peak = jnp.maximum(peak, jnp.abs(smoothed))
        page_ref[0, 12 + block : 13 + block, :] = jnp.max(peak.T, axis=0, keepdims=True)
    page = page_ref[0]
    for peer in range(1, page_ref.shape[0]):
        page_ref[peer] = page


def serve_kernel(lengths_ref, blocks_ref, pages_ref, served_hbm, scale_ref, tok_ref, served_ref, sems):
    low = lax.broadcasted_iota(jnp.int32, (24, 128), 1) < 64

    def store(step):
        columns = pl.ds(1536 * step, 1536)
        return pltpu.make_async_copy(served_ref.at[:, columns], served_hbm.at[:, columns], sems.at[step])

    for step in range(8):
        for pair in range(4 * step, 4 * step + 4):
            even = pages_ref[2 * pair].astype(jnp.float32)
            odd = pages_ref[2 * pair + 1].astype(jnp.float32)
            upper = jnp.where(low, even[48:72], odd[48:72])
            lower = pltpu.roll(jnp.where(low, odd[48:72], even[48:72]), 64, 1)
            middle = jnp.concatenate([upper, lower], axis=0)
            for part, tile in enumerate((even[0:48], middle, odd[0:48])):
                row = 3 * pair + part
                scale = blocks_ref[row // 12, row % 12 : row % 12 + 1, :]
                served_ref[:, pl.ds(128 * row, 128)] = (tile * scale).astype(jnp.bfloat16)
        store(step).start()
    scale_ref[...] = blocks_ref[lax.axis_index("mp"), 0:12, :]
    peaks = jnp.max(blocks_ref[:, 12:16, :], axis=0)
    lane = lax.broadcasted_iota(jnp.int32, (1, 128), 1)
    for block in range(4):
        valid = lane + 128 * (block % 2) < lengths_ref[block // 2]
        tok_ref[block : block + 1, :] = jnp.where(valid, peaks[block : block + 1], 0.0)
    for step in range(8):
        store(step).wait()


def swap(x, axis, bit):
    size = lax.axis_size(axis)
    return lax.ppermute(x, axis, [(i, i ^ bit) for i in range(size)])


def body(acts, lengths, ln_gain, ln_bias, w_fc1):
    gain = ln_gain.reshape(12, 128)
    bias = ln_bias.reshape(12, 128)
    with jax.named_scope("weight_exchange"):
        packed = pl.pallas_call(
            pack_kernel,
            out_shape=jax.ShapeDtypeStruct((64, 72, 128), jnp.bfloat16),
            in_specs=[ANY_SPEC],
            out_specs=ANY_SPEC,
            scratch_shapes=[
                pltpu.VMEM((192, 3072), jnp.bfloat16),
                pltpu.VMEM((64, 72, 128), jnp.bfloat16),
                pltpu.SemaphoreType.DMA((8,)),
                pltpu.SemaphoreType.DMA((8,)),
            ],
            compiler_params=params(60),
        )(w_fc1)
        pages = lax.all_to_all(packed, "dp", 0, 0, tiled=True)
    with jax.named_scope("token_moments"):
        sums = pl.pallas_call(
            stats_kernel,
            out_shape=jax.ShapeDtypeStruct((16, 128), jnp.float32),
            in_specs=[VMEM_SPEC, VMEM_SPEC],
            out_specs=VMEM_SPEC,
            scratch_shapes=[pltpu.VMEM((384, 128), jnp.float32)],
            compiler_params=params(),
        )(acts, w_fc1)
        added = lax.broadcasted_iota(jnp.int32, (16, 128), 0) < 8
        for bit in (1, 2, 4):
            other = swap(sums, "mp", bit)
            sums = jnp.where(added, sums + other, jnp.maximum(sums, other))
    with jax.named_scope("channel_maxima"):
        maxima = pl.pallas_call(
            act_kernel,
            out_shape=jax.ShapeDtypeStruct((16, 128), jnp.float32),
            in_specs=[SMEM_SPEC] + [VMEM_SPEC] * 4,
            out_specs=VMEM_SPEC,
            compiler_params=params(),
        )(lengths, sums, acts, gain, bias)
        maxima = jnp.maximum(maxima, swap(maxima, "dp", 1))
        maxima, pages = lax.optimization_barrier((maxima, pages))
        copies = jnp.broadcast_to(maxima[None], (32, 16, 128))
        kinds = [[2 * chip + core for chip in range(32)] for core in range(2)]
        maxima = lax.all_to_all(copies, "dp", 0, 0, axis_index_groups=kinds, tiled=True)
    with jax.named_scope("token_peaks"):
        page = pl.pallas_call(
            peak_kernel,
            out_shape=jax.ShapeDtypeStruct((8, 16, 128), jnp.float32),
            in_specs=[VMEM_SPEC] * 5,
            out_specs=VMEM_SPEC,
            compiler_params=params(),
        )(maxima, sums, acts, gain, bias)
        blocks = lax.all_to_all(page, "mp", 0, 0, tiled=True)
    with jax.named_scope("smoothed_weight"):
        served, scale, tok = pl.pallas_call(
            serve_kernel,
            out_shape=(
                jax.ShapeDtypeStruct((48, D), jnp.bfloat16),
                jax.ShapeDtypeStruct((12, 128), jnp.float32),
                jax.ShapeDtypeStruct((4, 128), jnp.float32),
            ),
            in_specs=[SMEM_SPEC, VMEM_SPEC, VMEM_SPEC],
            out_specs=(ANY_SPEC, VMEM_SPEC, VMEM_SPEC),
            scratch_shapes=[pltpu.VMEM((48, D), jnp.bfloat16), pltpu.SemaphoreType.DMA((8,))],
            compiler_params=params(),
        )(lengths, blocks, pages)
    return served, scale.reshape(1536), tok.reshape(512)


def solution(mesh):
    return jax.shard_map(
        body,
        mesh=mesh,
        in_specs=(P("dp", "mp"), P("dp"), P("mp"), P("mp"), P("dp", "mp")),
        out_specs=(P(("mp", "dp"), None), P("mp"), P("dp")),
        check_vma=False,
    )
```

```python
import jax
import jax.numpy as jnp
from jax import lax
from jax.experimental import pallas as pl
from jax.experimental.pallas import tpu as pltpu
from jax.sharding import PartitionSpec as P

D = 12288
SLOT = 256
EPS = 1e-05
VMEM_SPEC = pl.BlockSpec(memory_space=pltpu.VMEM)
SMEM_SPEC = pl.BlockSpec(memory_space=pltpu.SMEM)
ANY_SPEC = pl.BlockSpec(memory_space=pl.ANY)


def params(mebibytes=40):
    return pltpu.CompilerParams(vmem_limit_bytes=mebibytes * 1024 * 1024)


def pack_kernel(w_hbm, page_hbm, peak_ref, w_ref, page_ref, rows_ref, in_sems, out_sems):
    parity = lax.axis_index("dp") % 2
    low = lax.broadcasted_iota(jnp.int32, (24, 128), 1) < 64
    first = low == (parity == 0)

    def columns(step):
        return pl.ds(pl.multiple_of(384 * step, 128), 384)

    def fetch(step):
        return pltpu.make_async_copy(w_hbm.at[:, columns(step)], w_ref.at[:, columns(step)], in_sems.at[step])

    def store(step):
        peers = pl.ds(8 * step, 8)
        return pltpu.make_async_copy(page_ref.at[peers], page_hbm.at[peers], out_sems.at[step])

    for step in range(8):
        fetch(step).start()
    rows_ref[...] = jnp.zeros_like(rows_ref)

    def pack(step, carry):
        fetch(step).wait()
        full = w_ref[pl.ds(pl.multiple_of(64 * parity, 64), 128), columns(step)].T
        half = w_ref[pl.ds(pl.multiple_of(128 * (1 - parity), 64), 64), columns(step)]
        twice = jnp.concatenate([half, half], axis=0).T.astype(jnp.float32)
        for peer in range(8):
            upper = twice[48 * peer : 48 * peer + 24]
            lower = twice[48 * peer + 24 : 48 * peer + 48]
            halves = jnp.where(first, upper, lower).astype(jnp.bfloat16)
            page_ref[8 * step + peer] = jnp.concatenate([full[48 * peer : 48 * peer + 48], halves], axis=0)
        store(step).start()
        return carry

    lax.fori_loop(0, 8, pack, 0)
    peak = jnp.zeros((192, 128), jnp.bfloat16)
    for tile in range(24):
        peak = jnp.maximum(peak, jnp.abs(w_ref[:, pl.ds(128 * tile, 128)]))
    rows_ref[pl.ds(pl.multiple_of(192 * parity, 64), 192), :] = peak.astype(jnp.float32)
    for block in range(3):
        peak_ref[block : block + 1, :] = jnp.max(rows_ref[pl.ds(128 * block, 128), :].T, axis=0, keepdims=True)
    peak_ref[3:8, :] = jnp.zeros((5, 128), jnp.float32)
    for step in range(8):
        store(step).wait()


def stats_kernel(peak_ref, acts_ref, page_ref):
    page_ref[8:16, :] = peak_ref[...]
    for block in range(4):
        total = jnp.zeros((128, 128), jnp.float32)
        square = jnp.zeros((128, 128), jnp.float32)
        for tile in range(12):
            x = acts_ref[pl.ds(128 * block, 128), pl.ds(128 * tile, 128)].astype(jnp.float32)
            total = total + x
            square = square + x * x
        page_ref[block : block + 1, :] = jnp.sum(total.T, axis=0, keepdims=True)
        page_ref[4 + block : 5 + block, :] = jnp.sum(square.T, axis=0, keepdims=True)


def moments(sums):
    mean = sums[0:4] / D
    var = sums[4:8] / D - mean * mean
    rstd = lax.rsqrt(var + EPS)
    return jnp.concatenate([mean, rstd], axis=0).T


def act_kernel(lengths_ref, sums_ref, acts_ref, gain_ref, bias_ref, page_ref):
    columns = moments(sums_ref[...])
    place = lax.broadcasted_iota(jnp.int32, (16, 128), 0)
    most = [jnp.full((8, 128), -jnp.inf, jnp.float32)] * 12
    least = [jnp.full((8, 128), jnp.inf, jnp.float32)] * 12
    for group in range(32):
        block, row = group // 8, 16 * (group % 8)
        mean = jnp.broadcast_to(columns[row : row + 16, block : block + 1], (16, 128))
        rstd = jnp.broadcast_to(columns[row : row + 16, 4 + block : 5 + block], (16, 128))
        valid = place + 16 * (group % 16) < lengths_ref[group // 16]
        for tile in range(12):
            x = (acts_ref[pl.ds(16 * group, 16), pl.ds(128 * tile, 128)].astype(jnp.float32) - mean) * rstd
            high = jnp.where(valid, x, -jnp.inf)
            low = jnp.where(valid, x, jnp.inf)
            most[tile] = jnp.maximum(most[tile], jnp.maximum(high[0:8], high[8:16]))
            least[tile] = jnp.minimum(least[tile], jnp.minimum(low[0:8], low[8:16]))
    for tile in range(12):
        gain, bias = gain_ref[tile : tile + 1, :], bias_ref[tile : tile + 1, :]
        high = jnp.max(most[tile], axis=0, keepdims=True) * gain + bias
        low = jnp.min(least[tile], axis=0, keepdims=True) * gain + bias
        page_ref[tile : tile + 1, :] = jnp.maximum(jnp.abs(high), jnp.abs(low))
    page_ref[12:15, :] = sums_ref[8:11, :]
    page_ref[15:16, :] = jnp.zeros((1, 128), jnp.float32)


def peak_kernel(maxima_ref, sums_ref, acts_ref, gain_ref, bias_ref, page_ref):
    columns = moments(sums_ref[...])
    start = 4 * lax.axis_index("mp")
    act = jnp.max(maxima_ref[:, 0:12, :], axis=0)
    for slot in range(4):
        page_ref[0, 3 * slot : 3 * slot + 3, :] = maxima_ref[start + slot, 12:15, :]
    scale = jnp.sqrt(act + EPS) / jnp.sqrt(page_ref[0, 0:12, :] + EPS)
    page_ref[0, 0:12, :] = scale
    inverse = 1.0 / scale
    gain = gain_ref[...] * inverse
    bias = bias_ref[...] * inverse
    for block in range(4):
        mean = jnp.broadcast_to(columns[:, block : block + 1], (128, 128))
        rstd = jnp.broadcast_to(columns[:, 4 + block : 5 + block], (128, 128))
        peak = jnp.zeros((128, 128), jnp.float32)
        for tile in range(12):
            x = acts_ref[pl.ds(128 * block, 128), pl.ds(128 * tile, 128)].astype(jnp.float32)
            smoothed = (x - mean) * rstd * gain[tile : tile + 1] + bias[tile : tile + 1]
            peak = jnp.maximum(peak, jnp.abs(smoothed))
        page_ref[0, 12 + block : 13 + block, :] = jnp.max(peak.T, axis=0, keepdims=True)
    page = page_ref[0]
    for peer in range(1, page_ref.shape[0]):
        page_ref[peer] = page


def serve_kernel(lengths_ref, blocks_ref, pages_ref, served_hbm, scale_ref, tok_ref, served_ref, sems):
    low = lax.broadcasted_iota(jnp.int32, (24, 128), 1) < 64

    def store(step):
        columns = pl.ds(1536 * step, 1536)
        return pltpu.make_async_copy(served_ref.at[:, columns], served_hbm.at[:, columns], sems.at[step])

    for step in range(8):
        for pair in range(4 * step, 4 * step + 4):
            even = pages_ref[2 * pair].astype(jnp.float32)
            odd = pages_ref[2 * pair + 1].astype(jnp.float32)
            upper = jnp.where(low, even[48:72], odd[48:72])
            lower = pltpu.roll(jnp.where(low, odd[48:72], even[48:72]), 64, 1)
            middle = jnp.concatenate([upper, lower], axis=0)
            for part, tile in enumerate((even[0:48], middle, odd[0:48])):
                row = 3 * pair + part
                scale = blocks_ref[row // 12, row % 12 : row % 12 + 1, :]
                served_ref[:, pl.ds(128 * row, 128)] = (tile * scale).astype(jnp.bfloat16)
        store(step).start()
    scale_ref[...] = blocks_ref[lax.axis_index("mp"), 0:12, :]
    peaks = jnp.max(blocks_ref[:, 12:16, :], axis=0)
    lane = lax.broadcasted_iota(jnp.int32, (1, 128), 1)
    for block in range(4):
        valid = lane + 128 * (block % 2) < lengths_ref[block // 2]
        tok_ref[block : block + 1, :] = jnp.where(valid, peaks[block : block + 1], 0.0)
    for step in range(8):
        store(step).wait()


def swap(x, axis, bit):
    size = lax.axis_size(axis)
    return lax.ppermute(x, axis, [(i, i ^ bit) for i in range(size)])


def body(acts, lengths, ln_gain, ln_bias, w_fc1):
    gain = ln_gain.reshape(12, 128)
    bias = ln_bias.reshape(12, 128)
    with jax.named_scope("weight_exchange"):
        packed, w_peak = pl.pallas_call(
            pack_kernel,
            out_shape=(
                jax.ShapeDtypeStruct((64, 72, 128), jnp.bfloat16),
                jax.ShapeDtypeStruct((8, 128), jnp.float32),
            ),
            in_specs=[ANY_SPEC],
            out_specs=(ANY_SPEC, VMEM_SPEC),
            scratch_shapes=[
                pltpu.VMEM((192, 3072), jnp.bfloat16),
                pltpu.VMEM((64, 72, 128), jnp.bfloat16),
                pltpu.VMEM((384, 128), jnp.float32),
                pltpu.SemaphoreType.DMA((8,)),
                pltpu.SemaphoreType.DMA((8,)),
            ],
            compiler_params=params(60),
        )(w_fc1)
        pages = lax.all_to_all(packed, "dp", 0, 0, tiled=True)
    with jax.named_scope("token_moments"):
        sums = pl.pallas_call(
            stats_kernel,
            out_shape=jax.ShapeDtypeStruct((16, 128), jnp.float32),
            in_specs=[VMEM_SPEC, VMEM_SPEC],
            out_specs=VMEM_SPEC,
            compiler_params=params(),
        )(w_peak, acts)
        added = lax.broadcasted_iota(jnp.int32, (16, 128), 0) < 8
        for bit in (1, 2, 4):
            other = swap(sums, "mp", bit)
            sums = jnp.where(added, sums + other, jnp.maximum(sums, other))
    with jax.named_scope("channel_maxima"):
        maxima = pl.pallas_call(
            act_kernel,
            out_shape=jax.ShapeDtypeStruct((16, 128), jnp.float32),
            in_specs=[SMEM_SPEC] + [VMEM_SPEC] * 4,
            out_specs=VMEM_SPEC,
            compiler_params=params(),
        )(lengths, sums, acts, gain, bias)
        maxima = jnp.maximum(maxima, swap(maxima, "dp", 1))
        maxima, pages = lax.optimization_barrier((maxima, pages))
        copies = jnp.broadcast_to(maxima[None], (32, 16, 128))
        kinds = [[2 * chip + core for chip in range(32)] for core in range(2)]
        maxima = lax.all_to_all(copies, "dp", 0, 0, axis_index_groups=kinds, tiled=True)
    with jax.named_scope("token_peaks"):
        page = pl.pallas_call(
            peak_kernel,
            out_shape=jax.ShapeDtypeStruct((8, 16, 128), jnp.float32),
            in_specs=[VMEM_SPEC] * 5,
            out_specs=VMEM_SPEC,
            compiler_params=params(),
        )(maxima, sums, acts, gain, bias)
        blocks = lax.all_to_all(page, "mp", 0, 0, tiled=True)
    with jax.named_scope("smoothed_weight"):
        served, scale, tok = pl.pallas_call(
            serve_kernel,
            out_shape=(
                jax.ShapeDtypeStruct((48, D), jnp.bfloat16),
                jax.ShapeDtypeStruct((12, 128), jnp.float32),
                jax.ShapeDtypeStruct((4, 128), jnp.float32),
            ),
            in_specs=[SMEM_SPEC, VMEM_SPEC, VMEM_SPEC],
            out_specs=(ANY_SPEC, VMEM_SPEC, VMEM_SPEC),
            scratch_shapes=[pltpu.VMEM((48, D), jnp.bfloat16), pltpu.SemaphoreType.DMA((8,))],
            compiler_params=params(),
        )(lengths, blocks, pages)
    return served, scale.reshape(1536), tok.reshape(512)


def solution(mesh):
    return jax.shard_map(
        body,
        mesh=mesh,
        in_specs=(P("dp", "mp"), P("dp"), P("mp"), P("mp"), P("dp", "mp")),
        out_specs=(P(("mp", "dp"), None), P("mp"), P("dp")),
        check_vma=False,
    )
```

```python
import jax
import jax.numpy as jnp
from jax import lax
from jax.experimental import pallas as pl
from jax.experimental.pallas import tpu as pltpu
from jax.sharding import PartitionSpec as P

D = 12288
SLOT = 256
EPS = 1e-05
VMEM_SPEC = pl.BlockSpec(memory_space=pltpu.VMEM)
SMEM_SPEC = pl.BlockSpec(memory_space=pltpu.SMEM)
ANY_SPEC = pl.BlockSpec(memory_space=pl.ANY)


def params(mebibytes=40):
    return pltpu.CompilerParams(vmem_limit_bytes=mebibytes * 1024 * 1024)


def pack_kernel(w_hbm, page_hbm, peak_hbm, w_ref, page_ref, peak_ref, in_sems, out_sems, peak_sem):
    parity = lax.axis_index("dp") % 2
    low = lax.broadcasted_iota(jnp.int32, (24, 128), 1) < 64
    first = low == (parity == 0)

    def columns(step):
        return pl.ds(pl.multiple_of(384 * step, 128), 384)

    def fetch(step):
        return pltpu.make_async_copy(w_hbm.at[:, columns(step)], w_ref.at[:, columns(step)], in_sems.at[step])

    def store(step):
        peers = pl.ds(8 * step, 8)
        return pltpu.make_async_copy(page_ref.at[peers], page_hbm.at[peers], out_sems.at[step])

    for step in range(8):
        fetch(step).start()

    def pack(step, peak):
        fetch(step).wait()
        w = jnp.abs(w_ref[:, columns(step)])
        peak = jnp.maximum(peak, jnp.maximum(jnp.maximum(w[:, 0:128], w[:, 128:256]), w[:, 256:384]))
        full = w_ref[pl.ds(pl.multiple_of(64 * parity, 64), 128), columns(step)].T
        half = w_ref[pl.ds(pl.multiple_of(128 * (1 - parity), 64), 64), columns(step)]
        twice = jnp.concatenate([half, half], axis=0).T.astype(jnp.float32)
        for peer in range(8):
            upper = twice[48 * peer : 48 * peer + 24]
            lower = twice[48 * peer + 24 : 48 * peer + 48]
            halves = jnp.where(first, upper, lower).astype(jnp.bfloat16)
            page_ref[8 * step + peer] = jnp.concatenate([full[48 * peer : 48 * peer + 48], halves], axis=0)
        store(step).start()
        return peak

    peak_ref[...] = lax.fori_loop(0, 8, pack, jnp.zeros((192, 128), jnp.bfloat16))
    peak_copy = pltpu.make_async_copy(peak_ref, peak_hbm, peak_sem)
    peak_copy.start()
    for step in range(8):
        store(step).wait()
    peak_copy.wait()


def stats_kernel(peak_ref, acts_ref, page_ref, rows_ref):
    rows_ref[...] = jnp.zeros_like(rows_ref)
    own = pl.ds(pl.multiple_of(192 * (lax.axis_index("dp") % 2), 64), 192)
    rows_ref[own, :] = peak_ref[...].astype(jnp.float32)
    for block in range(3):
        page_ref[8 + block : 9 + block, :] = jnp.max(rows_ref[pl.ds(128 * block, 128), :].T, axis=0, keepdims=True)
    page_ref[11:16, :] = jnp.zeros((5, 128), jnp.float32)
    for block in range(4):
        total = jnp.zeros((128, 128), jnp.float32)
        square = jnp.zeros((128, 128), jnp.float32)
        for tile in range(12):
            x = acts_ref[pl.ds(128 * block, 128), pl.ds(128 * tile, 128)].astype(jnp.float32)
            total = total + x
            square = square + x * x
        page_ref[block : block + 1, :] = jnp.sum(total.T, axis=0, keepdims=True)
        page_ref[4 + block : 5 + block, :] = jnp.sum(square.T, axis=0, keepdims=True)


def moments(sums):
    mean = sums[0:4] / D
    var = sums[4:8] / D - mean * mean
    rstd = lax.rsqrt(var + EPS)
    return jnp.concatenate([mean, rstd], axis=0).T


def act_kernel(lengths_ref, sums_ref, acts_ref, gain_ref, bias_ref, page_ref):
    columns = moments(sums_ref[...])
    place = lax.broadcasted_iota(jnp.int32, (16, 128), 0)
    most = [jnp.full((8, 128), -jnp.inf, jnp.float32)] * 12
    least = [jnp.full((8, 128), jnp.inf, jnp.float32)] * 12
    for group in range(32):
        block, row = group // 8, 16 * (group % 8)
        mean = jnp.broadcast_to(columns[row : row + 16, block : block + 1], (16, 128))
        rstd = jnp.broadcast_to(columns[row : row + 16, 4 + block : 5 + block], (16, 128))
        valid = place + 16 * (group % 16) < lengths_ref[group // 16]
        for tile in range(12):
            x = (acts_ref[pl.ds(16 * group, 16), pl.ds(128 * tile, 128)].astype(jnp.float32) - mean) * rstd
            high = jnp.where(valid, x, -jnp.inf)
            low = jnp.where(valid, x, jnp.inf)
            most[tile] = jnp.maximum(most[tile], jnp.maximum(high[0:8], high[8:16]))
            least[tile] = jnp.minimum(least[tile], jnp.minimum(low[0:8], low[8:16]))
    for tile in range(12):
        gain, bias = gain_ref[tile : tile + 1, :], bias_ref[tile : tile + 1, :]
        high = jnp.max(most[tile], axis=0, keepdims=True) * gain + bias
        low = jnp.min(least[tile], axis=0, keepdims=True) * gain + bias
        page_ref[tile : tile + 1, :] = jnp.maximum(jnp.abs(high), jnp.abs(low))
    page_ref[12:15, :] = sums_ref[8:11, :]
    page_ref[15:16, :] = jnp.zeros((1, 128), jnp.float32)


def peak_kernel(maxima_ref, sums_ref, acts_ref, gain_ref, bias_ref, page_ref):
    columns = moments(sums_ref[...])
    start = 4 * lax.axis_index("mp")
    act = jnp.max(maxima_ref[:, 0:12, :], axis=0)
    for slot in range(4):
        page_ref[0, 3 * slot : 3 * slot + 3, :] = maxima_ref[start + slot, 12:15, :]
    scale = jnp.sqrt(act + EPS) / jnp.sqrt(page_ref[0, 0:12, :] + EPS)
    page_ref[0, 0:12, :] = scale
    inverse = 1.0 / scale
    gain = gain_ref[...] * inverse
    bias = bias_ref[...] * inverse
    for block in range(4):
        mean = jnp.broadcast_to(columns[:, block : block + 1], (128, 128))
        rstd = jnp.broadcast_to(columns[:, 4 + block : 5 + block], (128, 128))
        peak = jnp.zeros((128, 128), jnp.float32)
        for tile in range(12):
            x = acts_ref[pl.ds(128 * block, 128), pl.ds(128 * tile, 128)].astype(jnp.float32)
            smoothed = (x - mean) * rstd * gain[tile : tile + 1] + bias[tile : tile + 1]
            peak = jnp.maximum(peak, jnp.abs(smoothed))
        page_ref[0, 12 + block : 13 + block, :] = jnp.max(peak.T, axis=0, keepdims=True)
    page = page_ref[0]
    for peer in range(1, page_ref.shape[0]):
        page_ref[peer] = page


def serve_kernel(lengths_ref, blocks_ref, pages_ref, served_hbm, scale_ref, tok_ref, served_ref, sems):
    low = lax.broadcasted_iota(jnp.int32, (24, 128), 1) < 64

    def store(step):
        columns = pl.ds(1536 * step, 1536)
        return pltpu.make_async_copy(served_ref.at[:, columns], served_hbm.at[:, columns], sems.at[step])

    for step in range(8):
        for pair in range(4 * step, 4 * step + 4):
            even = pages_ref[2 * pair].astype(jnp.float32)
            odd = pages_ref[2 * pair + 1].astype(jnp.float32)
            upper = jnp.where(low, even[48:72], odd[48:72])
            lower = pltpu.roll(jnp.where(low, odd[48:72], even[48:72]), 64, 1)
            middle = jnp.concatenate([upper, lower], axis=0)
            for part, tile in enumerate((even[0:48], middle, odd[0:48])):
                row = 3 * pair + part
                scale = blocks_ref[row // 12, row % 12 : row % 12 + 1, :]
                served_ref[:, pl.ds(128 * row, 128)] = (tile * scale).astype(jnp.bfloat16)
        store(step).start()
    scale_ref[...] = blocks_ref[lax.axis_index("mp"), 0:12, :]
    peaks = jnp.max(blocks_ref[:, 12:16, :], axis=0)
    lane = lax.broadcasted_iota(jnp.int32, (1, 128), 1)
    for block in range(4):
        valid = lane + 128 * (block % 2) < lengths_ref[block // 2]
        tok_ref[block : block + 1, :] = jnp.where(valid, peaks[block : block + 1], 0.0)
    for step in range(8):
        store(step).wait()


def swap(x, axis, bit):
    size = lax.axis_size(axis)
    return lax.ppermute(x, axis, [(i, i ^ bit) for i in range(size)])


def body(acts, lengths, ln_gain, ln_bias, w_fc1):
    gain = ln_gain.reshape(12, 128)
    bias = ln_bias.reshape(12, 128)
    with jax.named_scope("weight_exchange"):
        packed, w_peak = pl.pallas_call(
            pack_kernel,
            out_shape=(
                jax.ShapeDtypeStruct((64, 72, 128), jnp.bfloat16),
                jax.ShapeDtypeStruct((192, 128), jnp.bfloat16),
            ),
            in_specs=[ANY_SPEC],
            out_specs=(ANY_SPEC, ANY_SPEC),
            scratch_shapes=[
                pltpu.VMEM((192, 3072), jnp.bfloat16),
                pltpu.VMEM((64, 72, 128), jnp.bfloat16),
                pltpu.VMEM((192, 128), jnp.bfloat16),
                pltpu.SemaphoreType.DMA((8,)),
                pltpu.SemaphoreType.DMA((8,)),
                pltpu.SemaphoreType.DMA,
            ],
            compiler_params=params(60),
        )(w_fc1)
        pages = lax.all_to_all(packed, "dp", 0, 0, tiled=True)
    with jax.named_scope("token_moments"):
        sums = pl.pallas_call(
            stats_kernel,
            out_shape=jax.ShapeDtypeStruct((16, 128), jnp.float32),
            in_specs=[VMEM_SPEC, VMEM_SPEC],
            out_specs=VMEM_SPEC,
            scratch_shapes=[pltpu.VMEM((384, 128), jnp.float32)],
            compiler_params=params(),
        )(w_peak, acts)
        added = lax.broadcasted_iota(jnp.int32, (16, 128), 0) < 8
        for bit in (1, 2, 4):
            other = swap(sums, "mp", bit)
            sums = jnp.where(added, sums + other, jnp.maximum(sums, other))
    with jax.named_scope("channel_maxima"):
        maxima = pl.pallas_call(
            act_kernel,
            out_shape=jax.ShapeDtypeStruct((16, 128), jnp.float32),
            in_specs=[SMEM_SPEC] + [VMEM_SPEC] * 4,
            out_specs=VMEM_SPEC,
            compiler_params=params(),
        )(lengths, sums, acts, gain, bias)
        maxima = jnp.maximum(maxima, swap(maxima, "dp", 1))
        maxima, pages = lax.optimization_barrier((maxima, pages))
        copies = jnp.broadcast_to(maxima[None], (32, 16, 128))
        kinds = [[2 * chip + core for chip in range(32)] for core in range(2)]
        maxima = lax.all_to_all(copies, "dp", 0, 0, axis_index_groups=kinds, tiled=True)
    with jax.named_scope("token_peaks"):
        page = pl.pallas_call(
            peak_kernel,
            out_shape=jax.ShapeDtypeStruct((8, 16, 128), jnp.float32),
            in_specs=[VMEM_SPEC] * 5,
            out_specs=VMEM_SPEC,
            compiler_params=params(),
        )(maxima, sums, acts, gain, bias)
        blocks = lax.all_to_all(page, "mp", 0, 0, tiled=True)
    with jax.named_scope("smoothed_weight"):
        served, scale, tok = pl.pallas_call(
            serve_kernel,
            out_shape=(
                jax.ShapeDtypeStruct((48, D), jnp.bfloat16),
                jax.ShapeDtypeStruct((12, 128), jnp.float32),
                jax.ShapeDtypeStruct((4, 128), jnp.float32),
            ),
            in_specs=[SMEM_SPEC, VMEM_SPEC, VMEM_SPEC],
            out_specs=(ANY_SPEC, VMEM_SPEC, VMEM_SPEC),
            scratch_shapes=[pltpu.VMEM((48, D), jnp.bfloat16), pltpu.SemaphoreType.DMA((8,))],
            compiler_params=params(),
        )(lengths, blocks, pages)
    return served, scale.reshape(1536), tok.reshape(512)


def solution(mesh):
    return jax.shard_map(
        body,
        mesh=mesh,
        in_specs=(P("dp", "mp"), P("dp"), P("mp"), P("mp"), P("dp", "mp")),
        out_specs=(P(("mp", "dp"), None), P("mp"), P("dp")),
        check_vma=False,
    )
```

```python
import jax
import jax.numpy as jnp
from jax import lax
from jax.experimental import pallas as pl
from jax.experimental.pallas import tpu as pltpu
from jax.sharding import PartitionSpec as P

D = 12288
SLOT = 256
EPS = 1e-05
VMEM_SPEC = pl.BlockSpec(memory_space=pltpu.VMEM)
SMEM_SPEC = pl.BlockSpec(memory_space=pltpu.SMEM)
ANY_SPEC = pl.BlockSpec(memory_space=pl.ANY)


def params(mebibytes=40):
    return pltpu.CompilerParams(vmem_limit_bytes=mebibytes * 1024 * 1024)


def pack_kernel(w_hbm, page_hbm, peak_hbm, w_ref, page_ref, peak_ref, in_sems, out_sems, peak_sem):
    parity = lax.axis_index("dp") % 2
    low = lax.broadcasted_iota(jnp.int32, (24, 128), 1) < 64
    first = low == (parity == 0)

    def columns(step):
        return pl.ds(pl.multiple_of(384 * step, 128), 384)

    def fetch(step):
        return pltpu.make_async_copy(w_hbm.at[:, columns(step)], w_ref.at[:, columns(step)], in_sems.at[step])

    def store(step):
        peers = pl.ds(8 * step, 8)
        return pltpu.make_async_copy(page_ref.at[peers], page_hbm.at[peers], out_sems.at[step])

    for step in range(8):
        fetch(step).start()

    def pack(step, peak):
        fetch(step).wait()
        w = jnp.abs(w_ref[:, columns(step)])
        peak = jnp.maximum(peak, jnp.maximum(jnp.maximum(w[:, 0:128], w[:, 128:256]), w[:, 256:384]))
        full = w_ref[pl.ds(pl.multiple_of(64 * parity, 64), 128), columns(step)].T
        half = w_ref[pl.ds(pl.multiple_of(128 * (1 - parity), 64), 64), columns(step)]
        twice = jnp.concatenate([half, half], axis=0).T.astype(jnp.float32)
        for peer in range(8):
            upper = twice[48 * peer : 48 * peer + 24]
            lower = twice[48 * peer + 24 : 48 * peer + 48]
            halves = jnp.where(first, upper, lower).astype(jnp.bfloat16)
            page_ref[8 * step + peer] = jnp.concatenate([full[48 * peer : 48 * peer + 48], halves], axis=0)
        store(step).start()
        return peak

    peak_ref[...] = lax.fori_loop(0, 8, pack, jnp.zeros((192, 128), jnp.bfloat16))
    peak_copy = pltpu.make_async_copy(peak_ref, peak_hbm, peak_sem)
    peak_copy.start()
    for step in range(8):
        store(step).wait()
    peak_copy.wait()


def stats_kernel(peak_ref, acts_ref, page_ref, rows_ref):
    rows_ref[...] = jnp.zeros_like(rows_ref)
    own = pl.ds(pl.multiple_of(192 * (lax.axis_index("dp") % 2), 64), 192)
    rows_ref[own, :] = peak_ref[...].astype(jnp.float32)
    for block in range(3):
        page_ref[8 + block : 9 + block, :] = jnp.max(rows_ref[pl.ds(128 * block, 128), :].T, axis=0, keepdims=True)
    page_ref[11:16, :] = jnp.zeros((5, 128), jnp.float32)
    for block in range(4):
        total = jnp.zeros((128, 128), jnp.float32)
        square = jnp.zeros((128, 128), jnp.float32)
        for tile in range(12):
            x = acts_ref[pl.ds(128 * block, 128), pl.ds(128 * tile, 128)].astype(jnp.float32)
            total = total + x
            square = square + x * x
        page_ref[block : block + 1, :] = jnp.sum(total.T, axis=0, keepdims=True)
        page_ref[4 + block : 5 + block, :] = jnp.sum(square.T, axis=0, keepdims=True)


def moments(sums):
    mean = sums[0:4] / D
    var = sums[4:8] / D - mean * mean
    rstd = lax.rsqrt(var + EPS)
    return jnp.concatenate([mean, rstd], axis=0).T


def act_kernel(lengths_ref, sums_ref, acts_ref, gain_ref, bias_ref, page_ref):
    columns = moments(sums_ref[...])
    place = lax.broadcasted_iota(jnp.int32, (16, 128), 0)
    most = [jnp.full((8, 128), -jnp.inf, jnp.float32)] * 12
    least = [jnp.full((8, 128), jnp.inf, jnp.float32)] * 12
    for group in range(32):
        block, row = group // 8, 16 * (group % 8)
        mean = jnp.broadcast_to(columns[row : row + 16, block : block + 1], (16, 128))
        rstd = jnp.broadcast_to(columns[row : row + 16, 4 + block : 5 + block], (16, 128))
        valid = place + 16 * (group % 16) < lengths_ref[group // 16]
        for tile in range(12):
            x = (acts_ref[pl.ds(16 * group, 16), pl.ds(128 * tile, 128)].astype(jnp.float32) - mean) * rstd
            high = jnp.where(valid, x, -jnp.inf)
            low = jnp.where(valid, x, jnp.inf)
            most[tile] = jnp.maximum(most[tile], jnp.maximum(high[0:8], high[8:16]))
            least[tile] = jnp.minimum(least[tile], jnp.minimum(low[0:8], low[8:16]))
    for tile in range(12):
        gain, bias = gain_ref[tile : tile + 1, :], bias_ref[tile : tile + 1, :]
        high = jnp.max(most[tile], axis=0, keepdims=True) * gain + bias
        low = jnp.min(least[tile], axis=0, keepdims=True) * gain + bias
        page_ref[tile : tile + 1, :] = jnp.maximum(jnp.abs(high), jnp.abs(low))
    page_ref[12:15, :] = sums_ref[8:11, :]
    page_ref[15:16, :] = jnp.zeros((1, 128), jnp.float32)


def peak_kernel(maxima_ref, sums_ref, acts_ref, gain_ref, bias_ref, page_ref):
    columns = moments(sums_ref[...])
    start = 4 * lax.axis_index("mp")
    act = jnp.max(maxima_ref[:, 0:12, :], axis=0)
    for slot in range(4):
        page_ref[0, 3 * slot : 3 * slot + 3, :] = maxima_ref[start + slot, 12:15, :]
    scale = jnp.sqrt(act + EPS) / jnp.sqrt(page_ref[0, 0:12, :] + EPS)
    page_ref[0, 0:12, :] = scale
    inverse = 1.0 / scale
    gain = gain_ref[...] * inverse
    bias = bias_ref[...] * inverse
    for block in range(4):
        mean = jnp.broadcast_to(columns[:, block : block + 1], (128, 128))
        rstd = jnp.broadcast_to(columns[:, 4 + block : 5 + block], (128, 128))
        peak = jnp.zeros((128, 128), jnp.float32)
        for tile in range(12):
            x = acts_ref[pl.ds(128 * block, 128), pl.ds(128 * tile, 128)].astype(jnp.float32)
            smoothed = (x - mean) * rstd * gain[tile : tile + 1] + bias[tile : tile + 1]
            peak = jnp.maximum(peak, jnp.abs(smoothed))
        page_ref[0, 12 + block : 13 + block, :] = jnp.max(peak.T, axis=0, keepdims=True)
    page = page_ref[0]
    for peer in range(1, page_ref.shape[0]):
        page_ref[peer] = page


def serve_kernel(lengths_ref, blocks_ref, own_ref, other_ref, served_hbm, scale_ref, tok_ref, served_ref, sems):
    core = lax.axis_index("dp") % 2
    first = (lax.broadcasted_iota(jnp.int32, (24, 128), 1) < 64) == (core == 0)

    def store(step):
        columns = pl.ds(1536 * step, 1536)
        return pltpu.make_async_copy(served_ref.at[:, columns], served_hbm.at[:, columns], sems.at[step])

    for step in range(8):
        for chip in range(4 * step, 4 * step + 4):
            own = own_ref[2 * chip + core].astype(jnp.float32)
            other = other_ref[chip].astype(jnp.float32)
            upper = jnp.where(first, own[48:72], other[48:72])
            lower = pltpu.roll(jnp.where(first, other[48:72], own[48:72]), 64, 1)
            even = jnp.where(core == 0, own[0:48], other[0:48])
            odd = jnp.where(core == 0, other[0:48], own[0:48])
            for part, tile in enumerate((even, jnp.concatenate([upper, lower], axis=0), odd)):
                row = 3 * chip + part
                scale = blocks_ref[row // 12, row % 12 : row % 12 + 1, :]
                served_ref[:, pl.ds(128 * row, 128)] = (tile * scale).astype(jnp.bfloat16)
        store(step).start()
    scale_ref[...] = blocks_ref[lax.axis_index("mp"), 0:12, :]
    peaks = jnp.max(blocks_ref[:, 12:16, :], axis=0)
    lane = lax.broadcasted_iota(jnp.int32, (1, 128), 1)
    for block in range(4):
        valid = lane + 128 * (block % 2) < lengths_ref[block // 2]
        tok_ref[block : block + 1, :] = jnp.where(valid, peaks[block : block + 1], 0.0)
    for step in range(8):
        store(step).wait()


def swap(x, axis, bit):
    size = lax.axis_size(axis)
    return lax.ppermute(x, axis, [(i, i ^ bit) for i in range(size)])


def body(acts, lengths, ln_gain, ln_bias, w_fc1):
    gain = ln_gain.reshape(12, 128)
    bias = ln_bias.reshape(12, 128)
    with jax.named_scope("weight_exchange"):
        packed, w_peak = pl.pallas_call(
            pack_kernel,
            out_shape=(
                jax.ShapeDtypeStruct((64, 72, 128), jnp.bfloat16),
                jax.ShapeDtypeStruct((192, 128), jnp.bfloat16),
            ),
            in_specs=[ANY_SPEC],
            out_specs=(ANY_SPEC, ANY_SPEC),
            scratch_shapes=[
                pltpu.VMEM((192, 3072), jnp.bfloat16),
                pltpu.VMEM((64, 72, 128), jnp.bfloat16),
                pltpu.VMEM((192, 128), jnp.bfloat16),
                pltpu.SemaphoreType.DMA((8,)),
                pltpu.SemaphoreType.DMA((8,)),
                pltpu.SemaphoreType.DMA,
            ],
            compiler_params=params(60),
        )(w_fc1)
        kinds = [[2 * chip + core for chip in range(32)] for core in range(2)]
        pages = lax.all_to_all(packed, "dp", 0, 0, axis_index_groups=kinds, tiled=True)
    with jax.named_scope("token_moments"):
        sums = pl.pallas_call(
            stats_kernel,
            out_shape=jax.ShapeDtypeStruct((16, 128), jnp.float32),
            in_specs=[VMEM_SPEC, VMEM_SPEC],
            out_specs=VMEM_SPEC,
            scratch_shapes=[pltpu.VMEM((384, 128), jnp.float32)],
            compiler_params=params(),
        )(w_peak, acts)
        added = lax.broadcasted_iota(jnp.int32, (16, 128), 0) < 8
        for bit in (1, 2, 4):
            other = swap(sums, "mp", bit)
            sums = jnp.where(added, sums + other, jnp.maximum(sums, other))
    with jax.named_scope("channel_maxima"):
        maxima = pl.pallas_call(
            act_kernel,
            out_shape=jax.ShapeDtypeStruct((16, 128), jnp.float32),
            in_specs=[SMEM_SPEC] + [VMEM_SPEC] * 4,
            out_specs=VMEM_SPEC,
            compiler_params=params(),
        )(lengths, sums, acts, gain, bias)
        maxima = jnp.maximum(maxima, swap(maxima, "dp", 1))
        maxima, pages = lax.optimization_barrier((maxima, pages))
        copies = jnp.broadcast_to(maxima[None], (32, 16, 128))
        maxima = lax.all_to_all(copies, "dp", 0, 0, axis_index_groups=kinds, tiled=True)
    with jax.named_scope("core_halves"):
        theirs = lax.dynamic_index_in_dim(pages.reshape(32, 2, 72, 128), 1 - lax.axis_index("dp") % 2, 1, keepdims=False)
        others = swap(theirs, "dp", 1)
        maxima, others = lax.optimization_barrier((maxima, others))
    with jax.named_scope("token_peaks"):
        page = pl.pallas_call(
            peak_kernel,
            out_shape=jax.ShapeDtypeStruct((8, 16, 128), jnp.float32),
            in_specs=[VMEM_SPEC] * 5,
            out_specs=VMEM_SPEC,
            compiler_params=params(),
        )(maxima, sums, acts, gain, bias)
        blocks = lax.all_to_all(page, "mp", 0, 0, tiled=True)
    with jax.named_scope("smoothed_weight"):
        served, scale, tok = pl.pallas_call(
            serve_kernel,
            out_shape=(
                jax.ShapeDtypeStruct((48, D), jnp.bfloat16),
                jax.ShapeDtypeStruct((12, 128), jnp.float32),
                jax.ShapeDtypeStruct((4, 128), jnp.float32),
            ),
            in_specs=[SMEM_SPEC, VMEM_SPEC, VMEM_SPEC, VMEM_SPEC],
            out_specs=(ANY_SPEC, VMEM_SPEC, VMEM_SPEC),
            scratch_shapes=[pltpu.VMEM((48, D), jnp.bfloat16), pltpu.SemaphoreType.DMA((8,))],
            compiler_params=params(),
        )(lengths, blocks, pages, others)
    return served, scale.reshape(1536), tok.reshape(512)


def solution(mesh):
    return jax.shard_map(
        body,
        mesh=mesh,
        in_specs=(P("dp", "mp"), P("dp"), P("mp"), P("mp"), P("dp", "mp")),
        out_specs=(P(("mp", "dp"), None), P("mp"), P("dp")),
        check_vma=False,
    )
```

```python
import jax
import jax.numpy as jnp
from jax import lax
from jax.experimental import pallas as pl
from jax.experimental.pallas import tpu as pltpu
from jax.sharding import PartitionSpec as P

D = 12288
SLOT = 256
EPS = 1e-05
VMEM_SPEC = pl.BlockSpec(memory_space=pltpu.VMEM)
SMEM_SPEC = pl.BlockSpec(memory_space=pltpu.SMEM)
ANY_SPEC = pl.BlockSpec(memory_space=pl.ANY)


def params(mebibytes=40):
    return pltpu.CompilerParams(vmem_limit_bytes=mebibytes * 1024 * 1024)


def pack_kernel(w_hbm, page_hbm, peak_hbm, w_ref, page_ref, peak_ref, in_sems, out_sems, peak_sem):
    parity = lax.axis_index("dp") % 2
    low = lax.broadcasted_iota(jnp.int32, (24, 128), 1) < 64
    first = low == (parity == 0)

    def columns(step):
        return pl.ds(pl.multiple_of(384 * step, 128), 384)

    def fetch(step):
        return pltpu.make_async_copy(w_hbm.at[:, columns(step)], w_ref.at[:, columns(step)], in_sems.at[step])

    def store(step):
        peers = pl.ds(8 * step, 8)
        return pltpu.make_async_copy(page_ref.at[peers], page_hbm.at[peers], out_sems.at[step])

    for step in range(8):
        fetch(step).start()

    def pack(step, peak):
        fetch(step).wait()
        w = jnp.abs(w_ref[:, columns(step)])
        peak = jnp.maximum(peak, jnp.maximum(jnp.maximum(w[:, 0:128], w[:, 128:256]), w[:, 256:384]))
        full = w_ref[pl.ds(pl.multiple_of(64 * parity, 64), 128), columns(step)].T
        half = w_ref[pl.ds(pl.multiple_of(128 * (1 - parity), 64), 64), columns(step)]
        twice = jnp.concatenate([half, half], axis=0).T.astype(jnp.float32)
        for peer in range(8):
            upper = twice[48 * peer : 48 * peer + 24]
            lower = twice[48 * peer + 24 : 48 * peer + 48]
            halves = jnp.where(first, upper, lower).astype(jnp.bfloat16)
            page_ref[8 * step + peer] = jnp.concatenate([full[48 * peer : 48 * peer + 48], halves], axis=0)
        store(step).start()
        return peak

    peak_ref[...] = lax.fori_loop(0, 8, pack, jnp.zeros((192, 128), jnp.bfloat16))
    peak_copy = pltpu.make_async_copy(peak_ref, peak_hbm, peak_sem)
    peak_copy.start()
    for step in range(8):
        store(step).wait()
    peak_copy.wait()


def stats_kernel(peak_ref, acts_ref, page_ref, rows_ref):
    rows_ref[...] = jnp.zeros_like(rows_ref)
    own = pl.ds(pl.multiple_of(192 * (lax.axis_index("dp") % 2), 64), 192)
    rows_ref[own, :] = peak_ref[...].astype(jnp.float32)
    for block in range(3):
        page_ref[8 + block : 9 + block, :] = jnp.max(rows_ref[pl.ds(128 * block, 128), :].T, axis=0, keepdims=True)
    page_ref[11:16, :] = jnp.zeros((5, 128), jnp.float32)
    for block in range(4):
        total = jnp.zeros((128, 128), jnp.float32)
        square = jnp.zeros((128, 128), jnp.float32)
        for tile in range(12):
            x = acts_ref[pl.ds(128 * block, 128), pl.ds(128 * tile, 128)].astype(jnp.float32)
            total = total + x
            square = square + x * x
        page_ref[block : block + 1, :] = jnp.sum(total.T, axis=0, keepdims=True)
        page_ref[4 + block : 5 + block, :] = jnp.sum(square.T, axis=0, keepdims=True)


def moments(sums):
    mean = sums[0:4] / D
    var = sums[4:8] / D - mean * mean
    rstd = lax.rsqrt(var + EPS)
    return jnp.concatenate([mean, rstd], axis=0).T


def act_kernel(lengths_ref, sums_ref, acts_ref, gain_ref, bias_ref, page_ref, mean_ref, rstd_ref):
    columns = moments(sums_ref[...])
    place = lax.broadcasted_iota(jnp.int32, (16, 128), 0)
    for block in range(4):
        mean_ref[128 * block : 128 * block + 128, :] = jnp.broadcast_to(columns[:, block : block + 1], (128, 128))
        rstd_ref[128 * block : 128 * block + 128, :] = jnp.broadcast_to(columns[:, 4 + block : 5 + block], (128, 128))

    def extend(group, carry):
        most, least = carry
        rows = pl.ds(pl.multiple_of(16 * group, 16), 16)
        mean, rstd = mean_ref[rows, :], rstd_ref[rows, :]
        valid = place + 16 * (group % 16) < lengths_ref[group // 16]
        highs, lows = [], []
        for tile in range(12):
            x = (acts_ref[rows, pl.ds(128 * tile, 128)].astype(jnp.float32) - mean) * rstd
            high = jnp.where(valid, x, -jnp.inf)
            low = jnp.where(valid, x, jnp.inf)
            highs.append(jnp.maximum(most[tile], jnp.maximum(high[0:8], high[8:16])))
            lows.append(jnp.minimum(least[tile], jnp.minimum(low[0:8], low[8:16])))
        return tuple(highs), tuple(lows)

    start = (
        tuple(jnp.full((8, 128), -jnp.inf, jnp.float32) for _ in range(12)),
        tuple(jnp.full((8, 128), jnp.inf, jnp.float32) for _ in range(12)),
    )
    most, least = lax.fori_loop(0, 32, extend, start)
    for tile in range(12):
        gain, bias = gain_ref[tile : tile + 1, :], bias_ref[tile : tile + 1, :]
        high = jnp.max(most[tile], axis=0, keepdims=True) * gain + bias
        low = jnp.min(least[tile], axis=0, keepdims=True) * gain + bias
        page_ref[tile : tile + 1, :] = jnp.maximum(jnp.abs(high), jnp.abs(low))
    page_ref[12:15, :] = sums_ref[8:11, :]
    page_ref[15:16, :] = jnp.zeros((1, 128), jnp.float32)


def peak_kernel(maxima_ref, sums_ref, acts_ref, gain_ref, bias_ref, page_ref, mean_ref, rstd_ref):
    columns = moments(sums_ref[...])
    start = 4 * lax.axis_index("mp")
    act = jnp.max(maxima_ref[:, 0:12, :], axis=0)
    for slot in range(4):
        page_ref[0, 3 * slot : 3 * slot + 3, :] = maxima_ref[start + slot, 12:15, :]
    scale = jnp.sqrt(act + EPS) / jnp.sqrt(page_ref[0, 0:12, :] + EPS)
    page_ref[0, 0:12, :] = scale
    inverse = 1.0 / scale
    gain = gain_ref[...] * inverse
    bias = bias_ref[...] * inverse
    for block in range(4):
        mean_ref[128 * block : 128 * block + 128, :] = jnp.broadcast_to(columns[:, block : block + 1], (128, 128))
        rstd_ref[128 * block : 128 * block + 128, :] = jnp.broadcast_to(columns[:, 4 + block : 5 + block], (128, 128))

    def find(block, carry):
        rows = pl.ds(pl.multiple_of(128 * block, 128), 128)
        mean, rstd = mean_ref[rows, :], rstd_ref[rows, :]
        peak = jnp.zeros((128, 128), jnp.float32)
        for tile in range(12):
            x = acts_ref[rows, pl.ds(128 * tile, 128)].astype(jnp.float32)
            smoothed = (x - mean) * rstd * gain[tile : tile + 1] + bias[tile : tile + 1]
            peak = jnp.maximum(peak, jnp.abs(smoothed))
        page_ref[0, pl.ds(12 + block, 1), :] = jnp.max(peak.T, axis=0, keepdims=True)
        return carry

    lax.fori_loop(0, 4, find, 0)
    page = page_ref[0]
    for peer in range(1, page_ref.shape[0]):
        page_ref[peer] = page


def serve_kernel(lengths_ref, blocks_ref, pages_ref, served_hbm, scale_ref, tok_ref, served_ref, sems):
    low = lax.broadcasted_iota(jnp.int32, (24, 128), 1) < 64

    def store(step):
        columns = pl.ds(pl.multiple_of(1536 * step, 128), 1536)
        return pltpu.make_async_copy(served_ref.at[:, columns], served_hbm.at[:, columns], sems.at[step])

    def serve(step, carry):
        for pair in range(4):
            even = pages_ref[8 * step + 2 * pair].astype(jnp.float32)
            odd = pages_ref[8 * step + 2 * pair + 1].astype(jnp.float32)
            upper = jnp.where(low, even[48:72], odd[48:72])
            lower = pltpu.roll(jnp.where(low, odd[48:72], even[48:72]), 64, 1)
            middle = jnp.concatenate([upper, lower], axis=0)
            for part, tile in enumerate((even[0:48], middle, odd[0:48])):
                row = 3 * pair + part
                columns = pl.ds(pl.multiple_of(1536 * step + 128 * row, 128), 128)
                served_ref[:, columns] = (tile * blocks_ref[step, row : row + 1, :]).astype(jnp.bfloat16)
        store(step).start()
        return carry

    lax.fori_loop(0, 8, serve, 0)
    scale_ref[...] = blocks_ref[lax.axis_index("mp"), 0:12, :]
    peaks = jnp.max(blocks_ref[:, 12:16, :], axis=0)
    lane = lax.broadcasted_iota(jnp.int32, (1, 128), 1)
    for block in range(4):
        valid = lane + 128 * (block % 2) < lengths_ref[block // 2]
        tok_ref[block : block + 1, :] = jnp.where(valid, peaks[block : block + 1], 0.0)
    for step in range(8):
        store(step).wait()


def swap(x, axis, bit):
    size = lax.axis_size(axis)
    return lax.ppermute(x, axis, [(i, i ^ bit) for i in range(size)])


def body(acts, lengths, ln_gain, ln_bias, w_fc1):
    gain = ln_gain.reshape(12, 128)
    bias = ln_bias.reshape(12, 128)
    with jax.named_scope("weight_exchange"):
        packed, w_peak = pl.pallas_call(
            pack_kernel,
            out_shape=(
                jax.ShapeDtypeStruct((64, 72, 128), jnp.bfloat16),
                jax.ShapeDtypeStruct((192, 128), jnp.bfloat16),
            ),
            in_specs=[ANY_SPEC],
            out_specs=(ANY_SPEC, ANY_SPEC),
            scratch_shapes=[
                pltpu.VMEM((192, 3072), jnp.bfloat16),
                pltpu.VMEM((64, 72, 128), jnp.bfloat16),
                pltpu.VMEM((192, 128), jnp.bfloat16),
                pltpu.SemaphoreType.DMA((8,)),
                pltpu.SemaphoreType.DMA((8,)),
                pltpu.SemaphoreType.DMA,
            ],
            compiler_params=params(60),
        )(w_fc1)
        pages = lax.all_to_all(packed, "dp", 0, 0, tiled=True)
    with jax.named_scope("token_moments"):
        sums = pl.pallas_call(
            stats_kernel,
            out_shape=jax.ShapeDtypeStruct((16, 128), jnp.float32),
            in_specs=[VMEM_SPEC, VMEM_SPEC],
            out_specs=VMEM_SPEC,
            scratch_shapes=[pltpu.VMEM((384, 128), jnp.float32)],
            compiler_params=params(),
        )(w_peak, acts)
        added = lax.broadcasted_iota(jnp.int32, (16, 128), 0) < 8
        for bit in (1, 2, 4):
            other = swap(sums, "mp", bit)
            sums = jnp.where(added, sums + other, jnp.maximum(sums, other))
    with jax.named_scope("channel_maxima"):
        maxima = pl.pallas_call(
            act_kernel,
            out_shape=jax.ShapeDtypeStruct((16, 128), jnp.float32),
            in_specs=[SMEM_SPEC] + [VMEM_SPEC] * 4,
            out_specs=VMEM_SPEC,
            scratch_shapes=[pltpu.VMEM((512, 128), jnp.float32)] * 2,
            compiler_params=params(),
        )(lengths, sums, acts, gain, bias)
        maxima = jnp.maximum(maxima, swap(maxima, "dp", 1))
        maxima, pages = lax.optimization_barrier((maxima, pages))
        copies = jnp.broadcast_to(maxima[None], (32, 16, 128))
        kinds = [[2 * chip + core for chip in range(32)] for core in range(2)]
        maxima = lax.all_to_all(copies, "dp", 0, 0, axis_index_groups=kinds, tiled=True)
    with jax.named_scope("token_peaks"):
        page = pl.pallas_call(
            peak_kernel,
            out_shape=jax.ShapeDtypeStruct((8, 16, 128), jnp.float32),
            in_specs=[VMEM_SPEC] * 5,
            out_specs=VMEM_SPEC,
            scratch_shapes=[pltpu.VMEM((512, 128), jnp.float32)] * 2,
            compiler_params=params(),
        )(maxima, sums, acts, gain, bias)
        blocks = lax.all_to_all(page, "mp", 0, 0, tiled=True)
    with jax.named_scope("smoothed_weight"):
        served, scale, tok = pl.pallas_call(
            serve_kernel,
            out_shape=(
                jax.ShapeDtypeStruct((48, D), jnp.bfloat16),
                jax.ShapeDtypeStruct((12, 128), jnp.float32),
                jax.ShapeDtypeStruct((4, 128), jnp.float32),
            ),
            in_specs=[SMEM_SPEC, VMEM_SPEC, VMEM_SPEC],
            out_specs=(ANY_SPEC, VMEM_SPEC, VMEM_SPEC),
            scratch_shapes=[pltpu.VMEM((48, D), jnp.bfloat16), pltpu.SemaphoreType.DMA((8,))],
            compiler_params=params(),
        )(lengths, blocks, pages)
    return served, scale.reshape(1536), tok.reshape(512)


def solution(mesh):
    return jax.shard_map(
        body,
        mesh=mesh,
        in_specs=(P("dp", "mp"), P("dp"), P("mp"), P("mp"), P("dp", "mp")),
        out_specs=(P(("mp", "dp"), None), P("mp"), P("dp")),
        check_vma=False,
    )
```

```python
import jax
import jax.numpy as jnp
from jax import lax
from jax.experimental import pallas as pl
from jax.experimental.pallas import tpu as pltpu
from jax.sharding import PartitionSpec as P

D = 12288
SLOT = 256
EPS = 1e-05
VMEM_SPEC = pl.BlockSpec(memory_space=pltpu.VMEM)
SMEM_SPEC = pl.BlockSpec(memory_space=pltpu.SMEM)
ANY_SPEC = pl.BlockSpec(memory_space=pl.ANY)


def params(mebibytes=40):
    return pltpu.CompilerParams(vmem_limit_bytes=mebibytes * 1024 * 1024)


def pack_kernel(w_hbm, page_hbm, peak_hbm, w_ref, page_ref, peak_ref, in_sems, out_sems, peak_sem):
    parity = lax.axis_index("dp") % 2
    low = lax.broadcasted_iota(jnp.int32, (24, 128), 1) < 64
    first = low == (parity == 0)

    def columns(step):
        return pl.ds(pl.multiple_of(384 * step, 128), 384)

    def fetch(step):
        return pltpu.make_async_copy(w_hbm.at[:, columns(step)], w_ref.at[:, columns(step)], in_sems.at[step])

    def store(step):
        peers = pl.ds(8 * step, 8)
        return pltpu.make_async_copy(page_ref.at[peers], page_hbm.at[peers], out_sems.at[step])

    for step in range(8):
        fetch(step).start()

    def pack(step, peak):
        fetch(step).wait()
        w = jnp.abs(w_ref[:, columns(step)])
        peak = jnp.maximum(peak, jnp.maximum(jnp.maximum(w[:, 0:128], w[:, 128:256]), w[:, 256:384]))
        full = w_ref[pl.ds(pl.multiple_of(64 * parity, 64), 128), columns(step)].T
        half = w_ref[pl.ds(pl.multiple_of(128 * (1 - parity), 64), 64), columns(step)]
        twice = jnp.concatenate([half, half], axis=0).T.astype(jnp.float32)
        for peer in range(8):
            upper = twice[48 * peer : 48 * peer + 24]
            lower = twice[48 * peer + 24 : 48 * peer + 48]
            halves = jnp.where(first, upper, lower).astype(jnp.bfloat16)
            page_ref[8 * step + peer] = jnp.concatenate([full[48 * peer : 48 * peer + 48], halves], axis=0)
        store(step).start()
        return peak

    peak_ref[...] = lax.fori_loop(0, 8, pack, jnp.zeros((192, 128), jnp.bfloat16), unroll=True)
    peak_copy = pltpu.make_async_copy(peak_ref, peak_hbm, peak_sem)
    peak_copy.start()
    for step in range(8):
        store(step).wait()
    peak_copy.wait()


def stats_kernel(peak_ref, acts_ref, page_ref, rows_ref):
    rows_ref[...] = jnp.zeros_like(rows_ref)
    own = pl.ds(pl.multiple_of(192 * (lax.axis_index("dp") % 2), 64), 192)
    rows_ref[own, :] = peak_ref[...].astype(jnp.float32)
    for block in range(3):
        page_ref[8 + block : 9 + block, :] = jnp.max(rows_ref[pl.ds(128 * block, 128), :].T, axis=0, keepdims=True)
    page_ref[11:16, :] = jnp.zeros((5, 128), jnp.float32)
    for block in range(4):
        total = jnp.zeros((128, 128), jnp.float32)
        square = jnp.zeros((128, 128), jnp.float32)
        for tile in range(12):
            x = acts_ref[pl.ds(128 * block, 128), pl.ds(128 * tile, 128)].astype(jnp.float32)
            total = total + x
            square = square + x * x
        page_ref[block : block + 1, :] = jnp.sum(total.T, axis=0, keepdims=True)
        page_ref[4 + block : 5 + block, :] = jnp.sum(square.T, axis=0, keepdims=True)


def moments(sums):
    mean = sums[0:4] / D
    var = sums[4:8] / D - mean * mean
    rstd = lax.rsqrt(var + EPS)
    return jnp.concatenate([mean, rstd], axis=0).T


def act_kernel(lengths_ref, sums_ref, acts_ref, gain_ref, bias_ref, page_ref):
    columns = moments(sums_ref[...])
    place = lax.broadcasted_iota(jnp.int32, (16, 128), 0)
    most = [jnp.full((8, 128), -jnp.inf, jnp.float32)] * 12
    least = [jnp.full((8, 128), jnp.inf, jnp.float32)] * 12
    for group in range(32):
        block, row = group // 8, 16 * (group % 8)
        mean = jnp.broadcast_to(columns[row : row + 16, block : block + 1], (16, 128))
        rstd = jnp.broadcast_to(columns[row : row + 16, 4 + block : 5 + block], (16, 128))
        valid = place + 16 * (group % 16) < lengths_ref[group // 16]
        for tile in range(12):
            x = (acts_ref[pl.ds(16 * group, 16), pl.ds(128 * tile, 128)].astype(jnp.float32) - mean) * rstd
            high = jnp.where(valid, x, -jnp.inf)
            low = jnp.where(valid, x, jnp.inf)
            most[tile] = jnp.maximum(most[tile], jnp.maximum(high[0:8], high[8:16]))
            least[tile] = jnp.minimum(least[tile], jnp.minimum(low[0:8], low[8:16]))
    for tile in range(12):
        gain, bias = gain_ref[tile : tile + 1, :], bias_ref[tile : tile + 1, :]
        high = jnp.max(most[tile], axis=0, keepdims=True) * gain + bias
        low = jnp.min(least[tile], axis=0, keepdims=True) * gain + bias
        page_ref[tile : tile + 1, :] = jnp.maximum(jnp.abs(high), jnp.abs(low))
    page_ref[12:15, :] = sums_ref[8:11, :]
    page_ref[15:16, :] = jnp.zeros((1, 128), jnp.float32)


def peak_kernel(maxima_ref, sums_ref, acts_ref, gain_ref, bias_ref, page_ref):
    columns = moments(sums_ref[...])
    start = 4 * lax.axis_index("mp")
    act = jnp.max(maxima_ref[:, 0:12, :], axis=0)
    for slot in range(4):
        page_ref[0, 3 * slot : 3 * slot + 3, :] = maxima_ref[start + slot, 12:15, :]
    scale = jnp.sqrt(act + EPS) / jnp.sqrt(page_ref[0, 0:12, :] + EPS)
    page_ref[0, 0:12, :] = scale
    inverse = 1.0 / scale
    gain = gain_ref[...] * inverse
    bias = bias_ref[...] * inverse
    for block in range(4):
        mean = jnp.broadcast_to(columns[:, block : block + 1], (128, 128))
        rstd = jnp.broadcast_to(columns[:, 4 + block : 5 + block], (128, 128))
        peak = jnp.zeros((128, 128), jnp.float32)
        for tile in range(12):
            x = acts_ref[pl.ds(128 * block, 128), pl.ds(128 * tile, 128)].astype(jnp.float32)
            smoothed = (x - mean) * rstd * gain[tile : tile + 1] + bias[tile : tile + 1]
            peak = jnp.maximum(peak, jnp.abs(smoothed))
        page_ref[0, 12 + block : 13 + block, :] = jnp.max(peak.T, axis=0, keepdims=True)
    page = page_ref[0]
    for peer in range(1, page_ref.shape[0]):
        page_ref[peer] = page


def serve_kernel(lengths_ref, blocks_ref, pages_ref, served_hbm, scale_hbm, tok_hbm, served_ref, scale_ref, tok_ref, sems, scale_sem, tok_sem):
    low = lax.broadcasted_iota(jnp.int32, (24, 128), 1) < 64

    def store(step):
        columns = pl.ds(1536 * step, 1536)
        return pltpu.make_async_copy(served_ref.at[:, columns], served_hbm.at[:, columns], sems.at[step])

    scale_ref[...] = blocks_ref[lax.axis_index("mp"), 0:12, :]
    peaks = jnp.max(blocks_ref[:, 12:16, :], axis=0)
    lane = lax.broadcasted_iota(jnp.int32, (1, 128), 1)
    for block in range(4):
        valid = lane + 128 * (block % 2) < lengths_ref[block // 2]
        tok_ref[block : block + 1, :] = jnp.where(valid, peaks[block : block + 1], 0.0)
    scale_copy = pltpu.make_async_copy(scale_ref, scale_hbm, scale_sem)
    tok_copy = pltpu.make_async_copy(tok_ref, tok_hbm, tok_sem)
    scale_copy.start()
    tok_copy.start()
    for step in range(8):
        for pair in range(4 * step, 4 * step + 4):
            even = pages_ref[2 * pair].astype(jnp.float32)
            odd = pages_ref[2 * pair + 1].astype(jnp.float32)
            upper = jnp.where(low, even[48:72], odd[48:72])
            lower = pltpu.roll(jnp.where(low, odd[48:72], even[48:72]), 64, 1)
            middle = jnp.concatenate([upper, lower], axis=0)
            for part, tile in enumerate((even[0:48], middle, odd[0:48])):
                row = 3 * pair + part
                scale = blocks_ref[row // 12, row % 12 : row % 12 + 1, :]
                served_ref[:, pl.ds(128 * row, 128)] = (tile * scale).astype(jnp.bfloat16)
        store(step).start()
    for step in range(8):
        store(step).wait()
    scale_copy.wait()
    tok_copy.wait()


def swap(x, axis, bit):
    size = lax.axis_size(axis)
    return lax.ppermute(x, axis, [(i, i ^ bit) for i in range(size)])


def body(acts, lengths, ln_gain, ln_bias, w_fc1):
    gain = ln_gain.reshape(12, 128)
    bias = ln_bias.reshape(12, 128)
    with jax.named_scope("weight_exchange"):
        packed, w_peak = pl.pallas_call(
            pack_kernel,
            out_shape=(
                jax.ShapeDtypeStruct((64, 72, 128), jnp.bfloat16),
                jax.ShapeDtypeStruct((192, 128), jnp.bfloat16),
            ),
            in_specs=[ANY_SPEC],
            out_specs=(ANY_SPEC, ANY_SPEC),
            scratch_shapes=[
                pltpu.VMEM((192, 3072), jnp.bfloat16),
                pltpu.VMEM((64, 72, 128), jnp.bfloat16),
                pltpu.VMEM((192, 128), jnp.bfloat16),
                pltpu.SemaphoreType.DMA((8,)),
                pltpu.SemaphoreType.DMA((8,)),
                pltpu.SemaphoreType.DMA,
            ],
            compiler_params=params(60),
        )(w_fc1)
        pages = lax.all_to_all(packed, "dp", 0, 0, tiled=True)
    with jax.named_scope("token_moments"):
        sums = pl.pallas_call(
            stats_kernel,
            out_shape=jax.ShapeDtypeStruct((16, 128), jnp.float32),
            in_specs=[VMEM_SPEC, VMEM_SPEC],
            out_specs=VMEM_SPEC,
            scratch_shapes=[pltpu.VMEM((384, 128), jnp.float32)],
            compiler_params=params(),
        )(w_peak, acts)
        added = lax.broadcasted_iota(jnp.int32, (16, 128), 0) < 8
        for bit in (1, 2, 4):
            other = swap(sums, "mp", bit)
            sums = jnp.where(added, sums + other, jnp.maximum(sums, other))
    with jax.named_scope("channel_maxima"):
        maxima = pl.pallas_call(
            act_kernel,
            out_shape=jax.ShapeDtypeStruct((16, 128), jnp.float32),
            in_specs=[SMEM_SPEC] + [VMEM_SPEC] * 4,
            out_specs=VMEM_SPEC,
            compiler_params=params(),
        )(lengths, sums, acts, gain, bias)
        maxima = jnp.maximum(maxima, swap(maxima, "dp", 1))
        maxima, pages = lax.optimization_barrier((maxima, pages))
        copies = jnp.broadcast_to(maxima[None], (32, 16, 128))
        kinds = [[2 * chip + core for chip in range(32)] for core in range(2)]
        maxima = lax.all_to_all(copies, "dp", 0, 0, axis_index_groups=kinds, tiled=True)
    with jax.named_scope("token_peaks"):
        page = pl.pallas_call(
            peak_kernel,
            out_shape=jax.ShapeDtypeStruct((8, 16, 128), jnp.float32),
            in_specs=[VMEM_SPEC] * 5,
            out_specs=VMEM_SPEC,
            compiler_params=params(),
        )(maxima, sums, acts, gain, bias)
        blocks = lax.all_to_all(page, "mp", 0, 0, tiled=True)
    with jax.named_scope("smoothed_weight"):
        served, scale, tok = pl.pallas_call(
            serve_kernel,
            out_shape=(
                jax.ShapeDtypeStruct((48, D), jnp.bfloat16),
                jax.ShapeDtypeStruct((12, 128), jnp.float32),
                jax.ShapeDtypeStruct((4, 128), jnp.float32),
            ),
            in_specs=[SMEM_SPEC, VMEM_SPEC, VMEM_SPEC],
            out_specs=(ANY_SPEC,) * 3,
            scratch_shapes=[
                pltpu.VMEM((48, D), jnp.bfloat16),
                pltpu.VMEM((12, 128), jnp.float32),
                pltpu.VMEM((4, 128), jnp.float32),
                pltpu.SemaphoreType.DMA((8,)),
                pltpu.SemaphoreType.DMA,
                pltpu.SemaphoreType.DMA,
            ],
            compiler_params=params(),
        )(lengths, blocks, pages)
    return served, scale.reshape(1536), tok.reshape(512)


def solution(mesh):
    return jax.shard_map(
        body,
        mesh=mesh,
        in_specs=(P("dp", "mp"), P("dp"), P("mp"), P("mp"), P("dp", "mp")),
        out_specs=(P(("mp", "dp"), None), P("mp"), P("dp")),
        check_vma=False,
    )
```
